128 devices in a mesh: sector: 2 (over core), slab: 64 (over z, y, x).
Axes of the slice: x: 4, y: 4, z: 4, core: 2. Of those that a mesh axis runs over, the one named last changes fastest.
Arguments:
- mode_basis: bfloat16 [64, 65536], replicated, may hold values from -6 to 6
- mode_coeff: bfloat16 [2048, 64], P(('sector', 'slab')), may hold values from -3 to 3
- reflect: bfloat16 [2048], P(('sector', 'slab')), may hold values from 0.29882812 to 1.5
- tile_row: int32 [2048], P(('sector', 'slab')), may hold values from 0 to 8191, as said below
- tile_col: int32 [2048], P(('sector', 'slab')), may hold values from 0 to 7936
- slot_live: int32 [2048], P(('sector', 'slab')), may hold values 0 or 1
Outputs:
- focal_plane: float32 [2, 8192, 8192], P(None, ('sector', 'slab'))
The draws below stay inside these ranges and needn't reach their ends.
Inputs may be any that keep to these rules, and one draw needn't show every extreme that they name: Slot s belongs to the device at position s // 16 of the joined axes sector then slab; tile_row[s] // 128 equals (s // 16) % 64.
All inputs are finite; a program needn't handle non-finite values. No bound on the sum of `slot_live` on one device may be relied on, other than what follows from the above.
Results may differ from the reference program's by a relative error of at most 0.0007.
Values may be sent and summed in bfloat16 or wider, within the bound.
A program may use at most 192 MiB of HBM per device.

```python
import jax
import jax.numpy as jnp
from jax import lax

GRID = 8192
TILE = 256
MODES = 64
SLOTS = 16
ROWS = 128
SLOTS_ALL = 2048


def draw_tile_row(key, part):
    key = jax.random.fold_in(key, 11)
    slot_number = jnp.arange(SLOTS_ALL, dtype=jnp.int32)
    band_index = slot_number // SLOTS % (GRID // ROWS)
    within = jax.random.randint(key, (SLOTS_ALL,), 0, ROWS, dtype=jnp.int32)
    position = slot_number % SLOTS
    within = jnp.where(position == 0, ROWS - 1, jnp.where(position == 1, 0, within))
    return (band_index * ROWS + within).astype(jnp.int32)


def draw_tile_col(key, part):
    key = jax.random.fold_in(key, 23)
    slot_number = jnp.arange(SLOTS_ALL, dtype=jnp.int32)
    column = jax.random.randint(key, (SLOTS_ALL,), 0, GRID - TILE + 1, dtype=jnp.int32)
    position = slot_number % SLOTS
    column = jnp.where(position == 0, GRID - TILE, jnp.where(position == 1, 0, column))
    return column.astype(jnp.int32)


def place_ends(drawn, stream_key, least, high):
    extent = drawn.shape
    index_at = [jax.random.randint(jax.random.fold_in(stream_key, axis), (), 0, extent[axis]) for axis in range(len(extent))]
    drawn = drawn.at[tuple(index_at)].set(least)
    longest = extent.index(max(extent))
    index_at[longest] = (index_at[longest] + 1) % extent[longest]
    return drawn.at[tuple(index_at)].set(high)


def steps_of(rng, extent, pieces, smallest, top_value):
    def one(axis_at, shards_of):
        draws = jax.random.uniform(jax.random.fold_in(jax.random.fold_in(rng, 6), axis_at), (shards_of,), jnp.float32, smallest / len(pieces), top_value / len(pieces))
        return jnp.repeat(jnp.exp(draws), extent[axis_at] // shards_of).reshape((-1,) + (1,) * (len(extent) - axis_at - 1))

    factor_of = one(*pieces[0])
    for cut in pieces[1:]:
        factor_of = factor_of * one(*cut)
    return factor_of


def noise(stream_key, extent, scale, bound, split=(), kind=jnp.bfloat16):
    entries = jax.random.normal(stream_key, extent, jnp.float32) * scale
    if len(split) > 0:
        entries = steps_of(stream_key, extent, split, -0.22, 0.18) * entries
    return jnp.clip(entries, min=-bound, max=bound).astype(kind)


def setup_inputs(seed: int = 0) -> dict:
    key_list = jax.random.split(jax.random.key(seed), 7)
    mode_basis = noise(key_list[0], (MODES, TILE * TILE), 1.0, 6.0)
    mode_coeff = noise(key_list[1], (SLOTS_ALL, MODES), 0.5, 3.0, ((0, 128),))
    reflect = jnp.clip(0.29882812 + 1.2011719 * jax.random.uniform(key_list[2], (SLOTS_ALL,), jnp.float32) ** steps_of(key_list[2], (SLOTS_ALL,), ((0, 128),), -0.2, 0.2), 0.29882812, 1.5).astype(jnp.bfloat16)
    tile_row = draw_tile_row(jax.random.fold_in(key_list[6], 71), 0)
    tile_col = draw_tile_col(jax.random.fold_in(key_list[6], 71), 0)
    slot_live = place_ends((jax.random.randint(key_list[5], (SLOTS_ALL,), 0, 5) < 2).astype(jnp.int32), jax.random.fold_in(key_list[5], 1), 0, 1)
    return {"mode_basis": mode_basis, "mode_coeff": mode_coeff, "reflect": reflect, "tile_row": tile_row, "tile_col": tile_col, "slot_live": slot_live}


def hexagon(size):
    cells = jnp.arange(size, dtype=jnp.int32)
    across = jnp.abs(2 * cells - (size - 1))
    vertical = across[:, None]
    horizontal = across[None, :]
    radius = size - 2
    inside = (8 * vertical <= 7 * radius) & (7 * horizontal + 4 * vertical <= 7 * radius)
    return inside.astype(jnp.float32)


def render(mode_basis, mode_coeff, reflect, tile_row, tile_col, slot_live, base_row, height, width, tile_size):
    hex_mask = hexagon(tile_size)

    def deposit(slot_index, canvas):
        phases = jnp.dot(lax.dynamic_slice_in_dim(mode_coeff, slot_index, 1, 0), mode_basis, preferred_element_type=jnp.float32).reshape(tile_size, tile_size)
        weight = reflect[slot_index].astype(jnp.float32) * slot_live[slot_index].astype(jnp.float32) * hex_mask
        tile_piece = jnp.stack([weight * jnp.cos(phases), weight * jnp.sin(phases)])
        corner = (jnp.zeros((), jnp.int32), (tile_row[slot_index] - base_row).astype(jnp.int32), tile_col[slot_index].astype(jnp.int32))
        current = lax.dynamic_slice(canvas, corner, (2, tile_size, tile_size))
        return lax.dynamic_update_slice(canvas, current + tile_piece, corner)

    canvas = jnp.zeros((2, height, width), jnp.float32)
    return lax.fori_loop(0, mode_coeff.shape[0], deposit, canvas)


def reference(mode_basis, mode_coeff, reflect, tile_row, tile_col, slot_live):
    pupil_grid = render(mode_basis, mode_coeff, reflect, tile_row, tile_col, slot_live, 0, GRID + TILE, GRID, TILE)
    pupil = pupil_grid[0, :GRID] + 1j * pupil_grid[1, :GRID]
    focal = jnp.fft.fft2(pupil) / GRID
    return jnp.stack([jnp.real(focal).T, jnp.imag(focal).T]).astype(jnp.float32)
```

```python
import functools
import math

import jax
import jax.numpy as jnp
import ml_dtypes
import numpy as np
from jax import lax
from jax.experimental import pallas as pl
from jax.experimental.pallas import tpu as pltpu
from jax.sharding import PartitionSpec as P

GRID = 8192
TILE = 256
SLOTS = 16
MODES = 64
SLABS = 64
DEVICES = 128
LINES = GRID // DEVICES
BLOCKS = GRID // 128
NEAR = 6 * SLOTS
CHUNK = 16
CHUNKS = LINES // CHUNK
PAD = 16
HALF = 32
MESH = pl.DeviceIdType.MESH
F32 = jnp.float32
BF16 = jnp.bfloat16

LOW = 12.0
STEPS = 32766.0 / (LOW + 15.25)


def polynomial(values, powers):
    spots = np.cos(np.pi * (np.arange(400) + 0.5) / 800) * 0.5
    table = np.stack([spots**power for power in powers], axis=1)
    return [float(c) for c in np.linalg.lstsq(table, values(np.pi * spots), rcond=None)[0]]


SIN_TERMS = polynomial(np.sin, (1, 3, 5, 7, 9))
COS_TERMS = polynomial(np.cos, (0, 2, 4, 6, 8))


def halves(table):
    high = table.astype(ml_dtypes.bfloat16)
    low = (table - high.astype(np.float64)).astype(ml_dtypes.bfloat16)
    return high, low


def angles(left, right, total):
    turns = np.outer(np.arange(left), np.arange(right)) % total
    return 2.0 * math.pi * turns / total


def tables():
    first = angles(64, 64, 64)
    col_first = np.block([[np.cos(first), np.sin(first)], [-np.sin(first), np.cos(first)]])
    high, low = halves(col_first)
    col_first_both = np.concatenate([high, high], axis=1)
    twist = angles(64, 128, GRID)
    col_twist = np.stack([np.cos(twist), np.sin(twist)]).astype(np.float32)
    second = angles(128, 128, 128)
    col_second = np.concatenate(halves(np.concatenate([np.cos(second), np.sin(second)], axis=1)))
    row_first = np.stack(
        halves(np.block([[np.cos(second), -np.sin(second)], [np.sin(second), np.cos(second)]]))
    )
    last_high, last_low = halves(col_first / GRID)
    last_both = np.concatenate([last_high, last_high], axis=1)
    return (
        (col_first_both, low, col_twist, col_second, row_first, col_twist),
        (last_both, last_low),
    )


def split(value):
    high = value.astype(BF16)
    return high, (value - high.astype(F32)).astype(BF16)


def dot(left, right):
    return jnp.dot(left, right, preferred_element_type=F32)


def dot_lanes(left, right):
    return lax.dot_general(left, right, (((1,), (1,)), ((), ())), preferred_element_type=F32)


def gather_kernel(own_ref, near_ref, send_sem, recv_sem):
    sector = lax.axis_index("sector")
    slab = lax.axis_index("slab")
    barrier = pltpu.get_barrier_semaphore()
    others = [(flip, hop) for hop in range(3) for flip in range(2)][1:]
    for flip, hop in others:
        for step in {hop, -hop}:
            pl.semaphore_signal(
                barrier,
                inc=1,
                device_id=(lax.rem(sector + flip, 2), lax.rem(slab + step + SLABS, SLABS)),
                device_id_type=MESH,
            )
    near_ref[0, sector] = own_ref[...]
    pl.semaphore_wait(barrier, 9)
    copies = []
    for number, (flip, hop) in enumerate(others):
        copy = pltpu.make_async_remote_copy(
            src_ref=own_ref,
            dst_ref=near_ref.at[hop, sector],
            send_sem=send_sem.at[number],
            recv_sem=recv_sem.at[number],
            device_id=(lax.rem(sector + flip, 2), lax.rem(slab + hop, SLABS)),
            device_id_type=MESH,
        )
        copy.start()
        copies.append(copy)
    for copy in copies:
        copy.wait()


def gather_near(own):
    return pl.pallas_call(
        gather_kernel,
        out_shape=jax.ShapeDtypeStruct((3, 2, SLOTS, 128), F32),
        in_specs=[pl.BlockSpec(memory_space=pltpu.VMEM)],
        out_specs=pl.BlockSpec(memory_space=pltpu.VMEM),
        scratch_shapes=[pltpu.SemaphoreType.DMA((5,)), pltpu.SemaphoreType.DMA((5,))],
        compiler_params=pltpu.CompilerParams(collective_id=0, has_side_effects=True),
        name="gather_near",
    )(own)


def circle(phase):
    turns = phase * (0.5 / math.pi)
    part = turns - jnp.round(turns)
    square = part * part
    sine = SIN_TERMS[-1]
    for term in SIN_TERMS[-2::-1]:
        sine = sine * square + term
    sine = sine * part
    cosine = COS_TERMS[-1]
    for term in COS_TERMS[-2::-1]:
        cosine = cosine * square + term
    double = sine + sine
    return 1.0 - double * sine, double * cosine


BASIS_PARTS = 8


def render_kernel(
    slot_ref, coeff_ref, basis_hbm, field_hbm, basis, left, right, canvas, basis_sem, out_sem
):
    sector = lax.axis_index("sector")
    slab = lax.axis_index("slab")
    base_row = 2 * LINES * slab + LINES * sector
    width = TILE * TILE // BASIS_PARTS

    def basis_copy(part):
        columns = pl.ds(part * width, width)
        return pltpu.make_async_copy(
            basis_hbm.at[:, columns], basis.at[:, columns], basis_sem.at[part]
        )

    for part in range(BASIS_PARTS):
        basis_copy(part).start()
    canvas[...] = jnp.zeros_like(canvas)
    coeff = coeff_ref[:, :MODES].astype(BF16)
    rows_at = TILE // BASIS_PARTS
    for part in range(BASIS_PARTS):
        basis_copy(part).wait()
        outer = 0 if part < BASIS_PARTS // 2 else 2
        mix = jnp.concatenate([coeff[32 * outer : 32 * outer + 32], coeff[32:64]], axis=0)

        @pl.loop(0, rows_at // 4)
        def _(step):
            row = part * rows_at + step * 4
            columns = pl.ds(pl.multiple_of(row * TILE, 4 * TILE), 4 * TILE)
            phases = dot(mix, basis[:, columns])
            for extra in range(4):
                place = pl.ds(pl.multiple_of((row + extra + PAD) * 64, 64), 64)
                at = extra * TILE
                left[place, :] = phases[:, at : at + 128]
                right[place, :] = phases[:, at + 128 : at + 256]

    lane = lax.broadcasted_iota(jnp.int32, (1, 128), 1)
    down = lax.broadcasted_iota(jnp.int32, (HALF, 1), 0)
    reach = 7 * (TILE - 2)
    for part in range(LINES // HALF):
        rows = pl.ds(part * HALF, HALF)

        @pl.loop(0, NEAR)
        def _(slot):
            tile_row = slot_ref[slot, 1].astype(jnp.int32)
            column = slot_ref[slot, 2].astype(jnp.int32)
            weight = slot_ref[slot, 0] * slot_ref[slot, 3]
            top = part * HALF + base_row - tile_row
            inside = (top >= 17 - (HALF - 1)) & (top <= 238) & (slot_ref[slot, 3] > 0.0)

            @pl.when(inside)
            def _():
                held = lax.rem(slot, 64)
                block = column // 128
                shift = lax.rem(column, 128)
                start = (top + PAD) * 64 + held
                vertical = jnp.abs(2 * (top + down) - (TILE - 1))
                vertical = jnp.where(8 * vertical <= reach, 4 * vertical, 4 * reach)
                place = (lane - shift) & 127
                room_left = reach - 7 * ((TILE - 1) - 2 * place)
                room_right = reach - 7 * (2 * place + 1)
                fits_left = jnp.broadcast_to(vertical, (HALF, 128)) <= room_left
                fits_right = jnp.broadcast_to(vertical, (HALF, 128)) <= room_right
                wave = pltpu.roll(left[pl.ds(start, HALF, stride=64), :], shift, 1)
                left_cos, left_sin = circle(wave)
                wave = pltpu.roll(right[pl.ds(start, HALF, stride=64), :], shift, 1)
                right_cos, right_sin = circle(wave)
                kept = jnp.broadcast_to(lane >= shift, (HALF, 128))
                for comp, (one, two) in enumerate(
                    ((left_cos, right_cos), (left_sin, right_sin))
                ):
                    one = jnp.where(fits_left, one * weight, 0.0)
                    two = jnp.where(fits_right, two * weight, 0.0)
                    at = comp * (BLOCKS + 1) + block
                    canvas[at, rows, :] += jnp.where(kept, one, 0.0)
                    canvas[at + 1, rows, :] += jnp.where(kept, two, one)

                    @pl.when(shift > 0)
                    def _():
                        canvas[at + 2, rows, :] += jnp.where(kept, 0.0, two)

        for comp in range(2):
            pltpu.make_async_copy(
                canvas.at[pl.ds(comp * (BLOCKS + 1), BLOCKS), rows],
                field_hbm.at[pl.ds(comp * BLOCKS, BLOCKS), rows],
                out_sem.at[part, comp],
            ).start()
    for part in range(LINES // HALF):
        rows = pl.ds(part * HALF, HALF)
        for comp in range(2):
            pltpu.make_async_copy(
                canvas.at[pl.ds(comp * (BLOCKS + 1), BLOCKS), rows],
                field_hbm.at[pl.ds(comp * BLOCKS, BLOCKS), rows],
                out_sem.at[part, comp],
            ).wait()


def render(near, mode_basis):
    near = near.reshape(NEAR, 128)
    slots = near[:, MODES : MODES + 4]
    return pl.pallas_call(
        render_kernel,
        out_shape=jax.ShapeDtypeStruct((2 * BLOCKS, LINES, 128), F32),
        in_specs=[
            pl.BlockSpec(memory_space=pltpu.SMEM),
            pl.BlockSpec(memory_space=pltpu.VMEM),
            pl.BlockSpec(memory_space=pl.ANY),
        ],
        out_specs=pl.BlockSpec(memory_space=pl.ANY),
        scratch_shapes=[
            pltpu.VMEM((MODES, TILE * TILE), BF16),
            pltpu.VMEM(((TILE + 2 * PAD) * 64, 128), F32),
            pltpu.VMEM(((TILE + 2 * PAD) * 64, 128), F32),
            pltpu.VMEM((2 * (BLOCKS + 1) + 1, LINES, 128), F32),
            pltpu.SemaphoreType.DMA((BASIS_PARTS,)),
            pltpu.SemaphoreType.DMA((LINES // HALF, 2)),
        ],
        compiler_params=pltpu.CompilerParams(vmem_limit_bytes=44 << 20),
        name="render_rows",
    )(slots, near, mode_basis)


def encode(value):
    size = jnp.log(jnp.abs(value)) * (STEPS / math.log(2.0)) + (LOW * STEPS + 0.5)
    code = jnp.maximum(size, 0.0).astype(jnp.int32)
    return jnp.where(value < 0.0, -code, code)


def decode(code):
    size = jnp.abs(code).astype(F32) * (math.log(2.0) / STEPS) - LOW * math.log(2.0)
    value = jnp.exp(size)
    return jnp.where(code == 0, 0.0, jnp.where(code < 0, -value, value))


def exchange_kernel(
    field_hbm,
    col_first_both,
    col_first_low,
    col_twist,
    col_second,
    row_first,
    row_twist,
    mid_hbm,
    rows_in,
    wide,
    outbox,
    inbox,
    plain,
    staged,
    in_sem,
    send_sem,
    recv_sem,
    out_sem,
):
    sector = lax.axis_index("sector")
    slab = lax.axis_index("slab")
    me = sector * SLABS + slab
    source = 2 * slab + sector

    def fetch(chunk):
        return pltpu.make_async_copy(
            field_hbm.at[:, pl.ds(chunk * CHUNK, CHUNK)], rows_in.at[chunk], in_sem.at[chunk]
        )

    for chunk in range(CHUNKS):
        fetch(chunk).start()
    barrier = pltpu.get_barrier_semaphore()

    @pl.loop(1, DEVICES)
    def _(step):
        other = lax.rem(me + step, DEVICES)
        pl.semaphore_signal(
            barrier, inc=1, device_id=(other // SLABS, other % SLABS), device_id_type=MESH
        )

    for chunk in range(CHUNKS):
        fetch(chunk).wait()
        lines = rows_in.at[chunk].reshape(2 * BLOCKS * CHUNK, 128)
        codes = wide.reshape(DEVICES * CHUNK, 128)

        @pl.loop(0, CHUNK // 2)
        def _(step):
            both = jnp.concatenate(
                [lines[pl.ds(2 * step + e, 2 * BLOCKS, stride=CHUNK), :] for e in range(2)], axis=1
            )
            high, low = split(both)
            mid = dot(col_first_both[...], jnp.concatenate([high, low], axis=0))
            mid = mid + dot(col_first_low[...], high)
            highs, lows = [], []
            for e in range(2):
                real = mid[:64, 128 * e : 128 * e + 128]
                imag = mid[64:, 128 * e : 128 * e + 128]
                turned_real = real * col_twist[0] + imag * col_twist[1]
                turned_imag = imag * col_twist[0] - real * col_twist[1]
                real_high, real_low = split(turned_real)
                imag_high, imag_low = split(turned_imag)
                highs += [
                    jnp.concatenate([real_high, imag_high], axis=1),
                    jnp.concatenate([imag_high, -real_high], axis=1),
                ]
                lows += [
                    jnp.concatenate([real_low, imag_low], axis=1),
                    jnp.concatenate([imag_low, -real_low], axis=1),
                ]
            first = dot_lanes(col_second[...], jnp.concatenate(highs, axis=0))
            second = dot_lanes(col_second[:DEVICES, :], jnp.concatenate(lows, axis=0))
            done = encode(first[:DEVICES] + first[DEVICES:] + second)
            for e in range(2):
                codes[pl.ds(2 * step + e, DEVICES, stride=CHUNK), :] = done[
                    :, 128 * e : 128 * e + 128
                ]

        @pl.loop(0, DEVICES // 16)
        def _(step):
            some = pl.ds(step * 16, 16)
            outbox[chunk, some] = wide[some].astype(jnp.int16)

        if chunk == 0:
            pl.semaphore_wait(barrier, DEVICES - 1)

        @pl.loop(1, DEVICES)
        def _(step):
            other = lax.rem(me + step, DEVICES)
            pltpu.make_async_remote_copy(
                src_ref=outbox.at[chunk, other],
                dst_ref=inbox.at[chunk, source],
                send_sem=send_sem.at[chunk],
                recv_sem=recv_sem.at[chunk],
                device_id=(other // SLABS, other % SLABS),
                device_id_type=MESH,
            ).start()

        inbox[chunk, source] = outbox[chunk, me]

    def leave(chunk):
        return pltpu.make_async_copy(
            staged.at[chunk % 2],
            mid_hbm.at[:, pl.ds(chunk * CHUNK, CHUNK)],
            out_sem.at[chunk % 2],
        )

    for chunk in range(CHUNKS):
        most = inbox.at[chunk, pl.ds(0, DEVICES - 1)]
        pltpu.make_async_copy(most, most, recv_sem.at[chunk]).wait()
        if chunk >= 2:
            leave(chunk - 2).wait()

        @pl.loop(0, DEVICES // 16)
        def _(step):
            some = pl.ds(step * 16, 16)
            plain[some] = decode(inbox[chunk, some].astype(jnp.int32))

        values = plain.reshape(DEVICES * CHUNK, 128)

        @pl.loop(0, CHUNK // 4)
        def _(step):
            parts = []
            for e in range(4):
                turned = values[pl.ds(4 * step + e, DEVICES, stride=CHUNK), :].T
                parts.append(jnp.concatenate([turned[:64], turned[64:]], axis=1))
            high, low = split(jnp.concatenate(parts, axis=0))
            mid = dot(high, row_first[0]) + dot(high, row_first[1]) + dot(low, row_first[0])
            for e in range(4):
                line = pl.ds(chunk * CHUNK + 4 * step + e, 1)
                cos = row_twist[0, line, :]
                sin = row_twist[1, line, :]
                real = mid[64 * e : 64 * e + 64, :128]
                imag = mid[64 * e : 64 * e + 64, 128:]
                staged[chunk % 2, 0, 4 * step + e] = real * cos + imag * sin
                staged[chunk % 2, 1, 4 * step + e] = imag * cos - real * sin

        leave(chunk).start()

    for chunk in range(CHUNKS):
        most = outbox.at[chunk, pl.ds(0, DEVICES - 1)]
        pltpu.make_async_copy(most, most, send_sem.at[chunk]).wait()
    for chunk in range(CHUNKS - 2, CHUNKS):
        leave(chunk).wait()


def exchange(field, consts):
    vmem = pl.BlockSpec(memory_space=pltpu.VMEM)
    anywhere = pl.BlockSpec(memory_space=pl.ANY)
    return pl.pallas_call(
        exchange_kernel,
        out_shape=jax.ShapeDtypeStruct((2, LINES, LINES, 128), F32),
        in_specs=[anywhere] + [vmem] * len(consts),
        out_specs=anywhere,
        scratch_shapes=[
            pltpu.VMEM((CHUNKS, 2 * BLOCKS, CHUNK, 128), F32),
            pltpu.VMEM((DEVICES, CHUNK, 128), jnp.int32),
            pltpu.VMEM((CHUNKS, DEVICES, CHUNK, 128), jnp.int16),
            pltpu.VMEM((CHUNKS, DEVICES, CHUNK, 128), jnp.int16),
            pltpu.VMEM((DEVICES, CHUNK, 128), F32),
            pltpu.VMEM((2, 2, CHUNK, LINES, 128), F32),
            pltpu.SemaphoreType.DMA((CHUNKS,)),
            pltpu.SemaphoreType.DMA((CHUNKS,)),
            pltpu.SemaphoreType.DMA((CHUNKS,)),
            pltpu.SemaphoreType.DMA((2,)),
        ],
        compiler_params=pltpu.CompilerParams(
            collective_id=1, has_side_effects=True, vmem_limit_bytes=40 << 20
        ),
        name="exchange",
    )(field, *consts)


def finish_kernel(mid_ref, last_both, last_low, out_ref, turned):
    lines = mid_ref.reshape(2 * LINES * 8, 128)
    for pair in range(4):
        both = jnp.concatenate(
            [lines[pl.ds(2 * pair + e, 2 * LINES, stride=8), :] for e in range(2)], axis=1
        )
        high, low = split(both)
        done = dot(last_both[...], jnp.concatenate([high, low], axis=0))
        done = done + dot(last_low[...], high)
        for e in range(2):
            turned[pl.ds(2 * pair + e, 2 * LINES, stride=8), :] = done[:, 128 * e : 128 * e + 128]
    for comp in range(2):
        for block in range(LINES):
            at = (comp * LINES + block) * 8
            out_ref[comp, :, 128 * block : 128 * block + 128] = turned[at : at + 8, :]


def finish(mid, consts):
    return pl.pallas_call(
        finish_kernel,
        out_shape=jax.ShapeDtypeStruct((2, LINES, GRID), F32),
        grid=(LINES // 8,),
        in_specs=[
            pl.BlockSpec((2, LINES, 8, 128), lambda i: (0, 0, i, 0)),
            pl.BlockSpec((128, 256), lambda i: (0, 0)),
            pl.BlockSpec((128, 128), lambda i: (0, 0)),
        ],
        out_specs=pl.BlockSpec((2, 8, GRID), lambda i: (0, i, 0)),
        scratch_shapes=[pltpu.VMEM((2 * LINES * 8, 128), F32)],
        compiler_params=pltpu.CompilerParams(vmem_limit_bytes=24 << 20),
        name="finish",
    )(mid, *consts)


def body(mode_basis, mode_coeff, reflect, tile_row, tile_col, slot_live):
    scalars = jnp.stack([reflect.astype(F32), tile_row, tile_col, slot_live], axis=1)
    own = jnp.concatenate(
        [mode_coeff.astype(F32), scalars, jnp.zeros((SLOTS, 128 - MODES - 4), F32)], axis=1
    )
    first, last = tables()
    field = render(gather_near(own), mode_basis)
    mid = exchange(field, [jnp.asarray(t) for t in first])
    return finish(mid, [jnp.asarray(t) for t in last])


def solution(mesh):
    placed = (
        P(),
        P(("sector", "slab"), None),
        P(("sector", "slab")),
        P(("sector", "slab")),
        P(("sector", "slab")),
        P(("sector", "slab")),
    )
    return jax.shard_map(
        body,
        mesh=mesh,
        in_specs=placed,
        out_specs=P(None, ("sector", "slab"), None),
        check_vma=False,
    )
```

```python
import functools
import math

import jax
import jax.numpy as jnp
import ml_dtypes
import numpy as np
from jax import lax
from jax.experimental import pallas as pl
from jax.experimental.pallas import tpu as pltpu
from jax.sharding import PartitionSpec as P

GRID = 8192
TILE = 256
SLOTS = 16
MODES = 64
SLABS = 64
DEVICES = 128
LINES = GRID // DEVICES
BLOCKS = GRID // 128
NEAR = 6 * SLOTS
CHUNK = 16
CHUNKS = LINES // CHUNK
PAD = 16
HALF = 32
MESH = pl.DeviceIdType.MESH
F32 = jnp.float32
BF16 = jnp.bfloat16

LOW = 12.0
STEPS = 32766.0 / (LOW + 15.25)


def polynomial(values, powers):
    spots = np.cos(np.pi * (np.arange(400) + 0.5) / 800) * 0.5
    table = np.stack([spots**power for power in powers], axis=1)
    return [float(c) for c in np.linalg.lstsq(table, values(np.pi * spots), rcond=None)[0]]


SIN_TERMS = polynomial(np.sin, (1, 3, 5, 7, 9))
COS_TERMS = polynomial(np.cos, (0, 2, 4, 6, 8))


def halves(table):
    high = table.astype(ml_dtypes.bfloat16)
    low = (table - high.astype(np.float64)).astype(ml_dtypes.bfloat16)
    return high, low


def angles(left, right, total):
    turns = np.outer(np.arange(left), np.arange(right)) % total
    return 2.0 * math.pi * turns / total


def tables():
    first = angles(64, 64, 64)
    col_first = np.block([[np.cos(first), np.sin(first)], [-np.sin(first), np.cos(first)]])
    high, low = halves(col_first)
    col_first_both = np.concatenate([high, high], axis=1)
    twist = angles(64, 128, GRID)
    col_twist = np.stack([np.cos(twist), np.sin(twist)]).astype(np.float32)
    second = angles(128, 128, 128)
    row_first = np.stack(
        halves(np.block([[np.cos(second), -np.sin(second)], [np.sin(second), np.cos(second)]]))
    )
    last_high, last_low = halves(col_first / GRID)
    last_both = np.concatenate([last_high, last_high], axis=1)
    return (
        (col_first_both, low, col_twist, row_first, col_twist),
        (last_both, last_low),
    )


def split(value):
    high = value.astype(BF16)
    return high, (value - high.astype(F32)).astype(BF16)


def dot(left, right):
    return jnp.dot(left, right, preferred_element_type=F32)


def gather_kernel(
    coeff_ref, reflect_ref, row_ref, column_ref, live_ref, near_ref, own, own_sem, send_sem, recv_sem
):
    sector = lax.axis_index("sector")
    slab = lax.axis_index("slab")
    barrier = pltpu.get_barrier_semaphore()
    others = [(flip, hop) for hop in range(3) for flip in range(2)][1:]
    for flip, hop in others:
        for step in {hop, -hop}:
            pl.semaphore_signal(
                barrier,
                inc=1,
                device_id=(lax.rem(sector + flip, 2), lax.rem(slab + step + SLABS, SLABS)),
                device_id_type=MESH,
            )
    own[:SLOTS, :MODES] = coeff_ref[...].astype(F32)
    for number, ref in enumerate((reflect_ref, row_ref, column_ref, live_ref)):
        own[SLOTS + number : SLOTS + number + 1, :SLOTS] = ref[...].astype(F32)
    kept = pltpu.make_async_copy(own, near_ref.at[0, sector], own_sem)
    kept.start()
    pl.semaphore_wait(barrier, 9)
    copies = []
    for number, (flip, hop) in enumerate(others):
        copy = pltpu.make_async_remote_copy(
            src_ref=own,
            dst_ref=near_ref.at[hop, sector],
            send_sem=send_sem.at[number],
            recv_sem=recv_sem.at[number],
            device_id=(lax.rem(sector + flip, 2), lax.rem(slab + hop, SLABS)),
            device_id_type=MESH,
        )
        copy.start()
        copies.append(copy)
    kept.wait()
    for copy in copies:
        copy.wait()


def gather_near(mode_coeff, *lists):
    vmem = pl.BlockSpec(memory_space=pltpu.VMEM)
    return pl.pallas_call(
        gather_kernel,
        out_shape=jax.ShapeDtypeStruct((3, 2, SLOTS + 8, 128), F32),
        in_specs=[vmem] * 5,
        out_specs=pl.BlockSpec(memory_space=pl.ANY),
        scratch_shapes=[
            pltpu.VMEM((SLOTS + 8, 128), F32),
            pltpu.SemaphoreType.DMA,
            pltpu.SemaphoreType.DMA((5,)),
            pltpu.SemaphoreType.DMA((5,)),
        ],
        compiler_params=pltpu.CompilerParams(collective_id=0, has_side_effects=True),
        name="gather_near",
    )(mode_coeff, *(values.reshape(1, SLOTS) for values in lists))


def circle(phase):
    turns = phase * (0.5 / math.pi)
    part = turns - jnp.round(turns)
    square = part * part
    sine = SIN_TERMS[-1]
    for term in SIN_TERMS[-2::-1]:
        sine = sine * square + term
    sine = sine * part
    cosine = COS_TERMS[-1]
    for term in COS_TERMS[-2::-1]:
        cosine = cosine * square + term
    double = sine + sine
    return 1.0 - double * sine, double * cosine


BASIS_PARTS = 8
TOGETHER = 8


def render_kernel(
    near_hbm,
    basis_hbm,
    field_hbm,
    near,
    basis,
    left,
    right,
    canvas,
    slots,
    tasks,
    near_sem,
    slots_sem,
    basis_sem,
    out_sem,
):
    sector = lax.axis_index("sector")
    slab = lax.axis_index("slab")
    base_row = 2 * LINES * slab + LINES * sector
    width = TILE * TILE // BASIS_PARTS

    def basis_copy(part):
        columns = pl.ds(part * width, width)
        return pltpu.make_async_copy(
            basis_hbm.at[:, columns], basis.at[:, columns], basis_sem.at[part]
        )

    near_copy = pltpu.make_async_copy(near_hbm, near, near_sem)
    slots_copy = pltpu.make_async_copy(near_hbm.at[:, :, pl.ds(SLOTS, 8)], slots, slots_sem)
    slots_copy.start()
    near_copy.start()
    for part in range(BASIS_PARTS):
        basis_copy(part).start()
    canvas[...] = jnp.zeros_like(canvas)
    slots_copy.wait()

    def about(slot):
        hop = slot // (2 * SLOTS)
        side = slot // SLOTS % 2
        at = slot % SLOTS
        return [slots[hop, side, number, at] for number in range(4)]

    def collect(slot, counts):
        _, tile_row, _, live = about(slot)
        top = base_row - tile_row.astype(jnp.int32)
        found = []
        for part, count in enumerate(counts):
            start = top + part * HALF
            reaches = (start >= 17 - (HALF - 1)) & (start <= 238) & (live > 0.0)
            tasks[part, count] = slot
            found.append(count + reaches.astype(jnp.int32))
        return tuple(found)

    counts = lax.fori_loop(0, NEAR, collect, (0,) * (LINES // HALF))
    near_copy.wait()
    coeff = [
        jnp.concatenate([near[hop, side, :SLOTS, :MODES] for side in range(2)], axis=0).astype(BF16)
        for hop in range(3)
    ]
    rows_at = TILE // BASIS_PARTS
    for part in range(BASIS_PARTS):
        basis_copy(part).wait()
        mix = jnp.concatenate([coeff[0 if part < BASIS_PARTS // 2 else 2], coeff[1]], axis=0)

        @pl.loop(0, rows_at // TOGETHER)
        def _(step):
            row = part * rows_at + step * TOGETHER
            columns = pl.ds(pl.multiple_of(row * TILE, TOGETHER * TILE), TOGETHER * TILE)
            phases = dot(mix, basis[:, columns])
            for extra in range(TOGETHER):
                place = pl.ds(pl.multiple_of((row + extra + PAD) * 64, 64), 64)
                at = extra * TILE
                left[place, :] = phases[:, at : at + 128]
                right[place, :] = phases[:, at + 128 : at + 256]

    lane = lax.broadcasted_iota(jnp.int32, (1, 128), 1)
    down = lax.broadcasted_iota(jnp.int32, (HALF, 1), 0)
    reach = 7 * (TILE - 2)

    def tile_part(slot, part, counted):
        reflectivity, tile_row, column, live = about(slot)
        weight = jnp.where(counted, reflectivity * live, 0.0)
        column = column.astype(jnp.int32)
        top = part * HALF + base_row - tile_row.astype(jnp.int32)
        block = column // 128
        shift = lax.rem(column, 128)
        start = (top + PAD) * 64 + lax.rem(slot, 64)
        vertical = jnp.abs(2 * (top + down) - (TILE - 1))
        vertical = jnp.where(8 * vertical <= reach, 4 * vertical, 4 * reach)
        vertical = jnp.broadcast_to(vertical, (HALF, 128))
        place = (lane - shift) & 127
        room_left = reach - 7 * ((TILE - 1) - 2 * place)
        room_right = reach - 7 * (2 * place + 1)
        both = []
        for ref, room in ((left, room_left), (right, room_right)):
            wave = pltpu.roll(ref[pl.ds(start, HALF, stride=64), :], shift, 1)
            amplitude = jnp.where(vertical <= room, weight, 0.0)
            inside = amplitude > 0.0
            cosine, sine = circle(wave)
            both.append(
                (
                    jnp.where(inside, cosine * amplitude, 0.0),
                    jnp.where(inside, sine * amplitude, 0.0),
                )
            )
        return block, jnp.broadcast_to(lane >= shift, (HALF, 128)), both

    for part in range(LINES // HALF):
        rows = pl.ds(part * HALF, HALF)
        count = counts[part]

        @pl.loop(0, (count + 1) // 2)
        def _(step):
            pieces = []
            for extra in range(2):
                at = 2 * step + extra
                pieces.append(tile_part(tasks[part, jnp.minimum(at, count - 1)], part, at < count))
            for block, kept, both in pieces:
                for comp in range(2):
                    one, two = both[0][comp], both[1][comp]
                    at = comp * (BLOCKS + 1) + block
                    canvas[at, rows, :] += jnp.where(kept, one, 0.0)
                    canvas[at + 1, rows, :] += jnp.where(kept, two, one)
                    canvas[at + 2, rows, :] += jnp.where(kept, 0.0, two)

        for comp in range(2):
            pltpu.make_async_copy(
                canvas.at[pl.ds(comp * (BLOCKS + 1), BLOCKS), rows],
                field_hbm.at[pl.ds(comp * BLOCKS, BLOCKS), rows],
                out_sem.at[part, comp],
            ).start()
    for part in range(LINES // HALF):
        rows = pl.ds(part * HALF, HALF)
        for comp in range(2):
            pltpu.make_async_copy(
                canvas.at[pl.ds(comp * (BLOCKS + 1), BLOCKS), rows],
                field_hbm.at[pl.ds(comp * BLOCKS, BLOCKS), rows],
                out_sem.at[part, comp],
            ).wait()


def render(near, mode_basis):
    anywhere = pl.BlockSpec(memory_space=pl.ANY)
    return pl.pallas_call(
        render_kernel,
        out_shape=jax.ShapeDtypeStruct((2 * BLOCKS, LINES, 128), F32),
        in_specs=[anywhere, anywhere],
        out_specs=anywhere,
        scratch_shapes=[
            pltpu.VMEM((3, 2, SLOTS + 8, 128), F32),
            pltpu.VMEM((MODES, TILE * TILE), BF16),
            pltpu.VMEM(((TILE + 2 * PAD) * 64, 128), F32),
            pltpu.VMEM(((TILE + 2 * PAD) * 64, 128), F32),
            pltpu.VMEM((2 * (BLOCKS + 1), LINES, 128), F32),
            pltpu.SMEM((3, 2, 8, 128), F32),
            pltpu.SMEM((LINES // HALF, NEAR), jnp.int32),
            pltpu.SemaphoreType.DMA,
            pltpu.SemaphoreType.DMA,
            pltpu.SemaphoreType.DMA((BASIS_PARTS,)),
            pltpu.SemaphoreType.DMA((LINES // HALF, 2)),
        ],
        compiler_params=pltpu.CompilerParams(vmem_limit_bytes=44 << 20),
        name="render_rows",
    )(near, mode_basis)


def encode(value):
    size = jnp.log(jnp.abs(value)) * (STEPS / math.log(2.0)) + (LOW * STEPS + 0.5)
    code = jnp.maximum(size, 0.0).astype(jnp.int32)
    return jnp.where(value < 0.0, -code, code)


def decode(code):
    size = jnp.abs(code).astype(F32) * (math.log(2.0) / STEPS) - LOW * math.log(2.0)
    value = jnp.exp(size)
    return jnp.where(code == 0, 0.0, jnp.where(code < 0, -value, value))


def exchange_kernel(
    field_hbm,
    col_first_both,
    col_first_low,
    col_twist,
    row_first,
    row_twist,
    mid_hbm,
    rows_in,
    wide,
    outbox,
    inbox,
    plain,
    staged,
    in_sem,
    send_sem,
    recv_sem,
    out_sem,
):
    sector = lax.axis_index("sector")
    slab = lax.axis_index("slab")
    me = sector * SLABS + slab
    source = 2 * slab + sector

    def fetch(chunk):
        return pltpu.make_async_copy(
            field_hbm.at[:, pl.ds(chunk * CHUNK, CHUNK)], rows_in.at[chunk], in_sem.at[chunk]
        )

    for chunk in range(CHUNKS):
        fetch(chunk).start()
    barrier = pltpu.get_barrier_semaphore()

    @pl.loop(1, DEVICES)
    def _(step):
        other = lax.rem(me + step, DEVICES)
        pl.semaphore_signal(
            barrier, inc=1, device_id=(other // SLABS, other % SLABS), device_id_type=MESH
        )

    for chunk in range(CHUNKS):
        fetch(chunk).wait()
        lines = rows_in.at[chunk].reshape(2 * BLOCKS * CHUNK, 128)
        codes = wide.reshape(DEVICES * CHUNK, 128)

        @pl.loop(0, CHUNK // 4)
        def _(step):
            parts = []
            for pair in range(2):
                both = jnp.concatenate(
                    [
                        lines[pl.ds(4 * step + 2 * pair + e, 2 * BLOCKS, stride=CHUNK), :]
                        for e in range(2)
                    ],
                    axis=1,
                )
                high, low = split(both)
                mid = dot(col_first_both[...], jnp.concatenate([high, low], axis=0))
                mid = mid + dot(col_first_low[...], high)
                for e in range(2):
                    real = mid[:64, 128 * e : 128 * e + 128]
                    imag = mid[64:, 128 * e : 128 * e + 128]
                    turned_real = real * col_twist[0] + imag * col_twist[1]
                    turned_imag = imag * col_twist[0] - real * col_twist[1]
                    parts.append(jnp.concatenate([turned_real, turned_imag], axis=1))
            high, low = split(jnp.concatenate(parts, axis=0))
            done = dot(high, row_first[0]) + dot(high, row_first[1]) + dot(low, row_first[0])
            done = encode(done)
            for e in range(4):
                some = done[64 * e : 64 * e + 64]
                some = jnp.concatenate([some[:, :128], some[:, 128:]], axis=0).T
                codes[pl.ds(4 * step + e, DEVICES, stride=CHUNK), :] = some

        @pl.loop(0, DEVICES // 16)
        def _(step):
            some = pl.ds(step * 16, 16)
            outbox[chunk, some] = wide[some].astype(jnp.int16)

        if chunk == 0:
            pl.semaphore_wait(barrier, DEVICES - 1)

        @pl.loop(1, DEVICES)
        def _(step):
            other = lax.rem(me + step, DEVICES)
            pltpu.make_async_remote_copy(
                src_ref=outbox.at[chunk, other],
                dst_ref=inbox.at[chunk, source],
                send_sem=send_sem.at[chunk],
                recv_sem=recv_sem.at[chunk],
                device_id=(other // SLABS, other % SLABS),
                device_id_type=MESH,
            ).start()

        inbox[chunk, source] = outbox[chunk, me]

    def leave(chunk):
        return pltpu.make_async_copy(
            staged.at[chunk % 2],
            mid_hbm.at[:, pl.ds(chunk * CHUNK, CHUNK)],
            out_sem.at[chunk % 2],
        )

    for chunk in range(CHUNKS):
        most = inbox.at[chunk, pl.ds(0, DEVICES - 1)]
        pltpu.make_async_copy(most, most, recv_sem.at[chunk]).wait()
        if chunk >= 2:
            leave(chunk - 2).wait()

        @pl.loop(0, DEVICES // 16)
        def _(step):
            some = pl.ds(step * 16, 16)
            plain[some] = decode(inbox[chunk, some].astype(jnp.int32))

        values = plain.reshape(DEVICES * CHUNK, 128)

        @pl.loop(0, CHUNK // 4)
        def _(step):
            parts = []
            for e in range(4):
                turned = values[pl.ds(4 * step + e, DEVICES, stride=CHUNK), :].T
                parts.append(jnp.concatenate([turned[:64], turned[64:]], axis=1))
            high, low = split(jnp.concatenate(parts, axis=0))
            mid = dot(high, row_first[0]) + dot(high, row_first[1]) + dot(low, row_first[0])
            for e in range(4):
                line = pl.ds(chunk * CHUNK + 4 * step + e, 1)
                cos = row_twist[0, line, :]
                sin = row_twist[1, line, :]
                real = mid[64 * e : 64 * e + 64, :128]
                imag = mid[64 * e : 64 * e + 64, 128:]
                staged[chunk % 2, 0, 4 * step + e] = real * cos + imag * sin
                staged[chunk % 2, 1, 4 * step + e] = imag * cos - real * sin

        leave(chunk).start()

    for chunk in range(CHUNKS):
        most = outbox.at[chunk, pl.ds(0, DEVICES - 1)]
        pltpu.make_async_copy(most, most, send_sem.at[chunk]).wait()
    for chunk in range(CHUNKS - 2, CHUNKS):
        leave(chunk).wait()


def exchange(field, consts):
    vmem = pl.BlockSpec(memory_space=pltpu.VMEM)
    anywhere = pl.BlockSpec(memory_space=pl.ANY)
    return pl.pallas_call(
        exchange_kernel,
        out_shape=jax.ShapeDtypeStruct((2, LINES, LINES, 128), F32),
        in_specs=[anywhere] + [vmem] * len(consts),
        out_specs=anywhere,
        scratch_shapes=[
            pltpu.VMEM((CHUNKS, 2 * BLOCKS, CHUNK, 128), F32),
            pltpu.VMEM((DEVICES, CHUNK, 128), jnp.int32),
            pltpu.VMEM((CHUNKS, DEVICES, CHUNK, 128), jnp.int16),
            pltpu.VMEM((CHUNKS, DEVICES, CHUNK, 128), jnp.int16),
            pltpu.VMEM((DEVICES, CHUNK, 128), F32),
            pltpu.VMEM((2, 2, CHUNK, LINES, 128), F32),
            pltpu.SemaphoreType.DMA((CHUNKS,)),
            pltpu.SemaphoreType.DMA((CHUNKS,)),
            pltpu.SemaphoreType.DMA((CHUNKS,)),
            pltpu.SemaphoreType.DMA((2,)),
        ],
        compiler_params=pltpu.CompilerParams(
            collective_id=1, has_side_effects=True, vmem_limit_bytes=40 << 20
        ),
        name="exchange",
    )(field, *consts)


def finish_kernel(mid_ref, last_both, last_low, out_ref, turned):
    lines = mid_ref.reshape(2 * LINES * 8, 128)
    for pair in range(4):
        both = jnp.concatenate(
            [lines[pl.ds(2 * pair + e, 2 * LINES, stride=8), :] for e in range(2)], axis=1
        )
        high, low = split(both)
        done = dot(last_both[...], jnp.concatenate([high, low], axis=0))
        done = done + dot(last_low[...], high)
        for e in range(2):
            turned[pl.ds(2 * pair + e, 2 * LINES, stride=8), :] = done[:, 128 * e : 128 * e + 128]
    for comp in range(2):
        for block in range(LINES):
            at = (comp * LINES + block) * 8
            out_ref[comp, :, 128 * block : 128 * block + 128] = turned[at : at + 8, :]


def finish(mid, consts):
    return pl.pallas_call(
        finish_kernel,
        out_shape=jax.ShapeDtypeStruct((2, LINES, GRID), F32),
        grid=(LINES // 8,),
        in_specs=[
            pl.BlockSpec((2, LINES, 8, 128), lambda i: (0, 0, i, 0)),
            pl.BlockSpec((128, 256), lambda i: (0, 0)),
            pl.BlockSpec((128, 128), lambda i: (0, 0)),
        ],
        out_specs=pl.BlockSpec((2, 8, GRID), lambda i: (0, i, 0)),
        scratch_shapes=[pltpu.VMEM((2 * LINES * 8, 128), F32)],
        compiler_params=pltpu.CompilerParams(vmem_limit_bytes=24 << 20),
        name="finish",
    )(mid, *consts)


def body(mode_basis, mode_coeff, reflect, tile_row, tile_col, slot_live):
    first, last = tables()
    near = gather_near(mode_coeff, reflect, tile_row, tile_col, slot_live)
    field = render(near, mode_basis)
    mid = exchange(field, [jnp.asarray(t) for t in first])
    return finish(mid, [jnp.asarray(t) for t in last])


def solution(mesh):
    placed = (
        P(),
        P(("sector", "slab"), None),
        P(("sector", "slab")),
        P(("sector", "slab")),
        P(("sector", "slab")),
        P(("sector", "slab")),
    )
    return jax.shard_map(
        body,
        mesh=mesh,
        in_specs=placed,
        out_specs=P(None, ("sector", "slab"), None),
        check_vma=False,
    )
```

```python
import functools
import math

import jax
import jax.numpy as jnp
import ml_dtypes
import numpy as np
from jax import lax
from jax.experimental import pallas as pl
from jax.experimental.pallas import tpu as pltpu
from jax.sharding import PartitionSpec as P

GRID = 8192
TILE = 256
SLOTS = 16
MODES = 64
SLABS = 64
DEVICES = 128
LINES = GRID // DEVICES
BLOCKS = GRID // 128
NEAR = 6 * SLOTS
CHUNK = 16
CHUNKS = LINES // CHUNK
PAD = 16
HALF = 32
MESH = pl.DeviceIdType.MESH
F32 = jnp.float32
BF16 = jnp.bfloat16

LOW = 12.0
STEPS = 32766.0 / (LOW + 15.25)


def polynomial(values, powers):
    spots = np.cos(np.pi * (np.arange(400) + 0.5) / 800) * 0.5
    table = np.stack([spots**power for power in powers], axis=1)
    return [float(c) for c in np.linalg.lstsq(table, values(np.pi * spots), rcond=None)[0]]


SIN_TERMS = polynomial(np.sin, (1, 3, 5, 7))
COS_TERMS = polynomial(np.cos, (0, 2, 4, 6))


def halves(table):
    high = table.astype(ml_dtypes.bfloat16)
    low = (table - high.astype(np.float64)).astype(ml_dtypes.bfloat16)
    return high, low


def angles(left, right, total):
    turns = np.outer(np.arange(left), np.arange(right)) % total
    return 2.0 * math.pi * turns / total


def stacked(table):
    high, low = halves(table)
    return np.block([[high, high], [low, np.zeros_like(low)]])


def tables():
    first = angles(64, 64, 64)
    turn = np.block([[np.cos(first), np.sin(first)], [-np.sin(first), np.cos(first)]])
    twist = angles(64, 128, GRID)
    second = angles(128, 128, 128)
    long_turn = np.block([[np.cos(second), -np.sin(second)], [np.sin(second), np.cos(second)]])
    return (
        stacked(turn),
        np.stack([np.cos(twist), np.sin(twist)]).astype(np.float32),
        np.stack(halves(long_turn)),
        stacked(turn / GRID),
    )


def split(value):
    high = value.astype(BF16)
    return high, (value - high.astype(F32)).astype(BF16)


def dot(left, right):
    return jnp.dot(left, right, preferred_element_type=F32)


def dot_short(table, value):
    high, low = split(value)
    both = dot(table, jnp.concatenate([high, low], axis=0))
    return both[:128] + both[128:]


def dot_long(value, tables):
    high, low = split(value)
    return dot(high, tables[0]) + dot(high, tables[1]) + dot(low, tables[0])


def gather_kernel(
    basis_hbm,
    coeff_hbm,
    reflect_hbm,
    row_hbm,
    column_hbm,
    live_hbm,
    near_ref,
    basis_ref,
    coeff_ref,
    reflect_ref,
    row_ref,
    column_ref,
    live_ref,
    own,
    basis_sem,
    in_sem,
    send_sem,
    recv_sem,
):
    sector = lax.axis_index("sector")
    slab = lax.axis_index("slab")
    barrier = pltpu.get_barrier_semaphore()
    sources = (coeff_hbm, reflect_hbm, row_hbm, column_hbm, live_hbm)
    held = (coeff_ref, reflect_ref, row_ref, column_ref, live_ref)
    loads = [
        pltpu.make_async_copy(one, two, in_sem.at[number])
        for number, (one, two) in enumerate(zip(sources, held))
    ]
    for load in loads:
        load.start()
    others = [(flip, hop) for hop in range(3) for flip in range(2)][1:]
    for flip, hop in others:
        for step in {hop, -hop}:
            pl.semaphore_signal(
                barrier,
                inc=1,
                device_id=(lax.rem(sector + flip, 2), lax.rem(slab + step + SLABS, SLABS)),
                device_id_type=MESH,
            )
    basis_copy = pltpu.make_async_copy(basis_hbm, basis_ref, basis_sem)
    basis_copy.start()
    for load in loads:
        load.wait()
    own[:SLOTS, :MODES] = coeff_ref[...].astype(F32)
    for number, ref in enumerate((reflect_ref, row_ref, column_ref, live_ref)):
        own[SLOTS + number : SLOTS + number + 1, :SLOTS] = ref[...].astype(F32)
    near_ref[0, sector] = own[...]
    pl.semaphore_wait(barrier, 9)
    copies = []
    for number, (flip, hop) in enumerate(others):
        copy = pltpu.make_async_remote_copy(
            src_ref=own,
            dst_ref=near_ref.at[hop, sector],
            send_sem=send_sem.at[number],
            recv_sem=recv_sem.at[number],
            device_id=(lax.rem(sector + flip, 2), lax.rem(slab + hop, SLABS)),
            device_id_type=MESH,
        )
        copy.start()
        copies.append(copy)
    for copy in copies:
        copy.wait()
    basis_copy.wait()


def gather_near(mode_basis, mode_coeff, *lists):
    vmem = pl.BlockSpec(memory_space=pltpu.VMEM)
    values = [mode_basis, mode_coeff] + [one.reshape(1, SLOTS) for one in lists]
    return pl.pallas_call(
        gather_kernel,
        out_shape=[
            jax.ShapeDtypeStruct((3, 2, SLOTS + 8, 128), F32),
            jax.ShapeDtypeStruct(mode_basis.shape, BF16),
        ],
        in_specs=[pl.BlockSpec(memory_space=pltpu.HBM)] * 6,
        out_specs=[vmem, vmem],
        scratch_shapes=[
            pltpu.VMEM((SLOTS, MODES), BF16),
            pltpu.VMEM((1, SLOTS), BF16),
            pltpu.VMEM((1, SLOTS), jnp.int32),
            pltpu.VMEM((1, SLOTS), jnp.int32),
            pltpu.VMEM((1, SLOTS), jnp.int32),
            pltpu.VMEM((SLOTS + 8, 128), F32),
            pltpu.SemaphoreType.DMA,
            pltpu.SemaphoreType.DMA((5,)),
            pltpu.SemaphoreType.DMA((5,)),
            pltpu.SemaphoreType.DMA((5,)),
        ],
        compiler_params=pltpu.CompilerParams(
            collective_id=0, has_side_effects=True, vmem_limit_bytes=20 << 20
        ),
        name="gather_near",
    )(*(pltpu.with_memory_space_constraint(value, pltpu.HBM) for value in values))


def circle(phase):
    turns = phase * (0.5 / math.pi)
    part = turns - jnp.round(turns)
    square = part * part
    sine = SIN_TERMS[-1]
    for term in SIN_TERMS[-2::-1]:
        sine = sine * square + term
    sine = sine * part
    cosine = COS_TERMS[-1]
    for term in COS_TERMS[-2::-1]:
        cosine = cosine * square + term
    double = sine + sine
    return 1.0 - double * sine, double * cosine


TOGETHER = 32


def render_kernel(near, basis, canvas, left, right, slots, tasks, slots_sem):
    sector = lax.axis_index("sector")
    slab = lax.axis_index("slab")
    base_row = 2 * LINES * slab + LINES * sector
    slots_copy = pltpu.make_async_copy(near.at[:, :, pl.ds(SLOTS, 8)], slots, slots_sem)
    slots_copy.start()
    canvas[...] = jnp.zeros_like(canvas)
    slots_copy.wait()

    def about(slot):
        hop = slot // (2 * SLOTS)
        side = slot // SLOTS % 2
        at = slot % SLOTS
        return [slots[hop, side, number, at] for number in range(4)]

    def collect(slot, counts):
        _, tile_row, _, live = about(slot)
        top = base_row - tile_row.astype(jnp.int32)
        found = []
        for part, count in enumerate(counts):
            start = top + part * HALF
            reaches = (start >= 17 - (HALF - 1)) & (start <= 238) & (live > 0.0)
            tasks[part, count] = slot
            found.append(count + reaches.astype(jnp.int32))
        return tuple(found)

    counts = lax.fori_loop(0, NEAR, collect, (0,) * (LINES // HALF))
    coeff = [
        jnp.concatenate([near[hop, side, :SLOTS, :MODES] for side in range(2)], axis=0).astype(BF16)
        for hop in range(3)
    ]
    for part in range(2):
        mix = jnp.concatenate([coeff[2 * part], coeff[1]], axis=0)

        @pl.loop(0, TILE // 2 // TOGETHER)
        def _(step):
            row = part * (TILE // 2) + step * TOGETHER
            columns = pl.ds(pl.multiple_of(row * TILE, TOGETHER * TILE), TOGETHER * TILE)
            phases = dot(mix, basis[:, columns])
            for extra in range(TOGETHER):
                place = pl.ds(pl.multiple_of((row + extra + PAD) * 64, 64), 64)
                at = extra * TILE
                left[place, :] = phases[:, at : at + 128]
                right[place, :] = phases[:, at + 128 : at + 256]

    lane = lax.broadcasted_iota(jnp.int32, (1, 128), 1)
    down = lax.broadcasted_iota(jnp.int32, (HALF, 1), 0)
    reach = 7 * (TILE - 2)

    def tile_part(slot, part, counted):
        reflectivity, tile_row, column, live = about(slot)
        weight = jnp.where(counted, reflectivity * live, 0.0)
        column = column.astype(jnp.int32)
        top = part * HALF + base_row - tile_row.astype(jnp.int32)
        block = column // 128
        shift = lax.rem(column, 128)
        start = (top + PAD) * 64 + lax.rem(slot, 64)
        vertical = jnp.abs(2 * (top + down) - (TILE - 1))
        vertical = jnp.where(8 * vertical <= reach, 4 * vertical, 4 * reach)
        vertical = jnp.broadcast_to(vertical, (HALF, 128))
        place = (lane - shift) & 127
        room_left = reach - 7 * ((TILE - 1) - 2 * place)
        room_right = reach - 7 * (2 * place + 1)
        both = []
        for ref, room in ((left, room_left), (right, room_right)):
            wave = pltpu.roll(ref[pl.ds(start, HALF, stride=64), :], shift, 1)
            inside = vertical <= room
            amplitude = jnp.where(inside, weight, 0.0)
            cosine, sine = circle(jnp.where(inside, wave, 0.0))
            both.append((cosine * amplitude, sine * amplitude))
        return block, jnp.broadcast_to(lane >= shift, (HALF, 128)), both

    for part in range(LINES // HALF):
        rows = pl.ds(part * HALF, HALF)
        count = counts[part]

        @pl.loop(0, (count + 1) // 2)
        def _(step):
            pieces = []
            for extra in range(2):
                at = 2 * step + extra
                pieces.append(tile_part(tasks[part, jnp.minimum(at, count - 1)], part, at < count))
            for block, kept, both in pieces:
                for comp in range(2):
                    one, two = both[0][comp], both[1][comp]
                    at = comp * BLOCKS + block
                    past = jnp.minimum(at + 2, 2 * BLOCKS - 1)
                    canvas[at, rows, :] += jnp.where(kept, one, 0.0)
                    canvas[at + 1, rows, :] += jnp.where(kept, two, one)
                    canvas[past, rows, :] += jnp.where(kept, 0.0, two)


def render(near, mode_basis):
    vmem = pl.BlockSpec(memory_space=pltpu.VMEM)
    return pl.pallas_call(
        render_kernel,
        out_shape=jax.ShapeDtypeStruct((2 * BLOCKS, LINES, 128), F32),
        in_specs=[vmem, vmem],
        out_specs=vmem,
        scratch_shapes=[
            pltpu.VMEM(((TILE + 2 * PAD) * 64, 128), F32),
            pltpu.VMEM(((TILE + 2 * PAD) * 64, 128), F32),
            pltpu.SMEM((3, 2, 8, 128), F32),
            pltpu.SMEM((LINES // HALF, NEAR), jnp.int32),
            pltpu.SemaphoreType.DMA,
        ],
        compiler_params=pltpu.CompilerParams(vmem_limit_bytes=40 << 20),
        name="render_rows",
    )(near, mode_basis)


def encode(value):
    size = jnp.log(jnp.abs(value)) * (STEPS / math.log(2.0)) + (LOW * STEPS + 0.5)
    code = jnp.maximum(size, 0.0).astype(jnp.int32)
    return jnp.where(value < 0.0, -code, code)


def decode(code):
    size = jnp.abs(code).astype(F32) * (math.log(2.0) / STEPS) - LOW * math.log(2.0)
    value = jnp.exp(size)
    return jnp.where(code == 0, 0.0, jnp.where(code < 0, -value, value))


def exchange_kernel(
    field, turn, twist, long_turn, mid_ref, wide, outbox, inbox, plain, send_sem, recv_sem
):
    sector = lax.axis_index("sector")
    slab = lax.axis_index("slab")
    me = sector * SLABS + slab
    source = 2 * slab + sector
    barrier = pltpu.get_barrier_semaphore()

    @pl.loop(1, DEVICES)
    def _(step):
        other = (me + step) & (DEVICES - 1)
        pl.semaphore_signal(
            barrier, inc=1, device_id=(other >> 6, other & (SLABS - 1)), device_id_type=MESH
        )

    lines = field.reshape(2 * BLOCKS * LINES, 128)
    codes = wide.reshape(DEVICES * CHUNK, 128)
    values = plain.reshape(DEVICES * CHUNK, 128)
    for chunk in range(CHUNKS):

        @pl.loop(0, CHUNK // 4)
        def _(step):
            parts = []
            for pair in range(2):
                line = chunk * CHUNK + 4 * step + 2 * pair
                both = [lines[pl.ds(line + e, 2 * BLOCKS, stride=LINES), :] for e in range(2)]
                mid = dot_short(turn[...], jnp.concatenate(both, axis=1))
                for e in range(2):
                    real = mid[:64, 128 * e : 128 * e + 128]
                    imag = mid[64:, 128 * e : 128 * e + 128]
                    turned_real = real * twist[0] + imag * twist[1]
                    turned_imag = imag * twist[0] - real * twist[1]
                    parts.append(jnp.concatenate([turned_real, turned_imag], axis=1))
            done = encode(dot_long(jnp.concatenate(parts, axis=0), long_turn))
            for e in range(4):
                some = done[64 * e : 64 * e + 64]
                some = jnp.concatenate([some[:, :128], some[:, 128:]], axis=0).T
                codes[pl.ds(4 * step + e, DEVICES, stride=CHUNK), :] = some

        @pl.loop(0, DEVICES // 16)
        def _(step):
            some = pl.ds(step * 16, 16)
            outbox[chunk, some] = wide[some].astype(jnp.int16)

        if chunk == 0:
            pl.semaphore_wait(barrier, DEVICES - 1)

        @pl.loop(1, DEVICES)
        def _(step):
            other = (me + step) & (DEVICES - 1)
            pltpu.make_async_remote_copy(
                src_ref=outbox.at[chunk, other],
                dst_ref=inbox.at[chunk, source],
                send_sem=send_sem.at[chunk],
                recv_sem=recv_sem.at[chunk],
                device_id=(other >> 6, other & (SLABS - 1)),
                device_id_type=MESH,
            ).start()

        inbox[chunk, source] = outbox[chunk, me]

    for chunk in range(CHUNKS):
        most = inbox.at[chunk, pl.ds(0, DEVICES - 1)]
        pltpu.make_async_copy(most, most, recv_sem.at[chunk]).wait()

        @pl.loop(0, DEVICES // 16)
        def _(step):
            some = pl.ds(step * 16, 16)
            plain[some] = decode(inbox[chunk, some].astype(jnp.int32))

        @pl.loop(0, CHUNK // 4)
        def _(step):
            parts = []
            for e in range(4):
                turned = values[pl.ds(4 * step + e, DEVICES, stride=CHUNK), :].T
                parts.append(jnp.concatenate([turned[:64], turned[64:]], axis=1))
            mid = dot_long(jnp.concatenate(parts, axis=0), long_turn)
            for e in range(4):
                line = chunk * CHUNK + 4 * step + e
                cos = twist[0, pl.ds(line, 1), :]
                sin = twist[1, pl.ds(line, 1), :]
                real = mid[64 * e : 64 * e + 64, :128]
                imag = mid[64 * e : 64 * e + 64, 128:]
                mid_ref[0, line] = real * cos + imag * sin
                mid_ref[1, line] = imag * cos - real * sin

    for chunk in range(CHUNKS):
        most = outbox.at[chunk, pl.ds(0, DEVICES - 1)]
        pltpu.make_async_copy(most, most, send_sem.at[chunk]).wait()


def exchange(field, *consts):
    vmem = pl.BlockSpec(memory_space=pltpu.VMEM)
    return pl.pallas_call(
        exchange_kernel,
        out_shape=jax.ShapeDtypeStruct((2, LINES, LINES, 128), F32),
        in_specs=[vmem] * 4,
        out_specs=vmem,
        scratch_shapes=[
            pltpu.VMEM((DEVICES, CHUNK, 128), jnp.int32),
            pltpu.VMEM((CHUNKS, DEVICES, CHUNK, 128), jnp.int16),
            pltpu.VMEM((CHUNKS, DEVICES, CHUNK, 128), jnp.int16),
            pltpu.VMEM((DEVICES, CHUNK, 128), F32),
            pltpu.SemaphoreType.DMA((CHUNKS,)),
            pltpu.SemaphoreType.DMA((CHUNKS,)),
        ],
        compiler_params=pltpu.CompilerParams(
            collective_id=1, has_side_effects=True, vmem_limit_bytes=32 << 20
        ),
        name="exchange",
    )(field, *consts)


def finish_kernel(mid_ref, turn, out_hbm, turned, ready, out_sem):
    lines = mid_ref.reshape(2 * LINES * LINES, 128)

    def leave(group):
        return pltpu.make_async_copy(
            ready.at[group % 2], out_hbm.at[:, pl.ds(group * 8, 8)], out_sem.at[group % 2]
        )

    for group in range(LINES // 8):
        for pair in range(4):
            line = group * 8 + 2 * pair
            both = [lines[pl.ds(line + e, 2 * LINES, stride=LINES), :] for e in range(2)]
            done = dot_short(turn[...], jnp.concatenate(both, axis=1))
            for e in range(2):
                turned[group % 2, pl.ds(2 * pair + e, 2 * LINES, stride=8), :] = done[
                    :, 128 * e : 128 * e + 128
                ]
        if group >= 2:
            leave(group - 2).wait()
        for comp in range(2):
            for block in range(LINES):
                at = (comp * LINES + block) * 8
                ready[group % 2, comp, :, 128 * block : 128 * block + 128] = turned[
                    group % 2, at : at + 8, :
                ]
        leave(group).start()
    for group in range(LINES // 8 - 2, LINES // 8):
        leave(group).wait()


def finish(mid, turn):
    vmem = pl.BlockSpec(memory_space=pltpu.VMEM)
    return pl.pallas_call(
        finish_kernel,
        out_shape=jax.ShapeDtypeStruct((2, LINES, GRID), F32),
        in_specs=[vmem, vmem],
        out_specs=pl.BlockSpec(memory_space=pl.ANY),
        scratch_shapes=[
            pltpu.VMEM((2, 2 * LINES * 8, 128), F32),
            pltpu.VMEM((2, 2, 8, GRID), F32),
            pltpu.SemaphoreType.DMA((2,)),
        ],
        compiler_params=pltpu.CompilerParams(vmem_limit_bytes=24 << 20),
        name="finish",
    )(mid, turn)


def body(mode_basis, mode_coeff, reflect, tile_row, tile_col, slot_live):
    turn, twist, long_turn, last_turn = (jnp.asarray(table) for table in tables())
    near, basis = gather_near(mode_basis, mode_coeff, reflect, tile_row, tile_col, slot_live)
    field = render(near, basis)
    mid = exchange(field, turn, twist, long_turn)
    return finish(mid, last_turn)


def solution(mesh):
    placed = (
        P(),
        P(("sector", "slab"), None),
        P(("sector", "slab")),
        P(("sector", "slab")),
        P(("sector", "slab")),
        P(("sector", "slab")),
    )
    return jax.shard_map(
        body,
        mesh=mesh,
        in_specs=placed,
        out_specs=P(None, ("sector", "slab"), None),
        check_vma=False,
    )
```

```python
import functools
import math

import jax
import jax.numpy as jnp
import ml_dtypes
import numpy as np
from jax import lax
from jax.experimental import pallas as pl
from jax.experimental.pallas import tpu as pltpu
from jax.sharding import PartitionSpec as P

GRID = 8192
TILE = 256
SLOTS = 16
MODES = 64
SLABS = 64
DEVICES = 128
LINES = GRID // DEVICES
BLOCKS = GRID // 128
NEAR = 6 * SLOTS
CHUNK = 16
CHUNKS = LINES // CHUNK
PAD = 16
HALF = 32
FIRST, LAST = 16, 240
WIDE = LINES + 8
SHORT = CHUNK + 8
MESH = pl.DeviceIdType.MESH
F32 = jnp.float32
BF16 = jnp.bfloat16

LOW = 12.0
STEPS = 32766.0 / (LOW + 15.25)


def polynomial(values, powers):
    spots = np.cos(np.pi * (np.arange(400) + 0.5) / 800) * 0.5
    table = np.stack([spots**power for power in powers], axis=1)
    return [float(c) for c in np.linalg.lstsq(table, values(np.pi * spots), rcond=None)[0]]


SIN_TERMS = polynomial(np.sin, (1, 3, 5, 7))
COS_TERMS = polynomial(np.cos, (0, 2, 4, 6))


def halves(table):
    high = table.astype(ml_dtypes.bfloat16)
    low = (table - high.astype(np.float64)).astype(ml_dtypes.bfloat16)
    return high, low


def angles(left, right, total):
    turns = np.outer(np.arange(left), np.arange(right)) % total
    return 2.0 * math.pi * turns / total


def stacked(table):
    high, low = halves(table)
    return np.block([[high, high], [low, np.zeros_like(low)]])


def tables():
    first = angles(64, 64, 64)
    turn = np.block([[np.cos(first), np.sin(first)], [-np.sin(first), np.cos(first)]])
    twist = angles(64, 128, GRID)
    second = angles(128, 128, 128)
    long_turn = np.block([[np.cos(second), -np.sin(second)], [np.sin(second), np.cos(second)]])
    return (
        stacked(turn),
        np.stack([np.cos(twist), np.sin(twist)]).astype(np.float32),
        np.stack(halves(long_turn)),
        stacked(turn / GRID),
    )


def split(value):
    high = value.astype(BF16)
    return high, (value - high.astype(F32)).astype(BF16)


def dot(left, right):
    return jnp.dot(left, right, preferred_element_type=F32)


def dot_short(table, value):
    high, low = split(value)
    both = dot(table, jnp.concatenate([high, low], axis=0))
    return both[:128] + both[128:]


def dot_long(value, tables):
    high, low = split(value)
    return dot(high, tables[0]) + dot(high, tables[1]) + dot(low, tables[0])


def gather_kernel(
    basis_hbm,
    coeff_hbm,
    reflect_hbm,
    row_hbm,
    column_hbm,
    live_hbm,
    near_ref,
    basis_ref,
    coeff_ref,
    reflect_ref,
    row_ref,
    column_ref,
    live_ref,
    own,
    basis_sem,
    in_sem,
    send_sem,
    recv_sem,
):
    sector = lax.axis_index("sector")
    slab = lax.axis_index("slab")
    barrier = pltpu.get_barrier_semaphore()
    used = pl.ds(FIRST * TILE, (LAST - FIRST) * TILE)
    basis_copy = pltpu.make_async_copy(basis_hbm.at[:, used], basis_ref, basis_sem)
    sources = (coeff_hbm, reflect_hbm, row_hbm, column_hbm, live_hbm)
    held = (coeff_ref, reflect_ref, row_ref, column_ref, live_ref)
    loads = [
        pltpu.make_async_copy(one, two, in_sem.at[number])
        for number, (one, two) in enumerate(zip(sources, held))
    ]
    for load in loads:
        load.start()
    basis_copy.start()
    others = [(flip, hop) for hop in range(3) for flip in range(2)][1:]
    for flip, hop in others:
        for step in {hop, -hop}:
            pl.semaphore_signal(
                barrier,
                inc=1,
                device_id=(lax.rem(sector + flip, 2), lax.rem(slab + step + SLABS, SLABS)),
                device_id_type=MESH,
            )
    for load in loads:
        load.wait()
    own[:SLOTS, :MODES] = coeff_ref[...].astype(F32)
    for number, ref in enumerate((reflect_ref, row_ref, column_ref, live_ref)):
        own[SLOTS + number : SLOTS + number + 1, :SLOTS] = ref[...].astype(F32)
    near_ref[0, sector] = own[...]
    pl.semaphore_wait(barrier, 9)
    copies = []
    for number, (flip, hop) in enumerate(others):
        copy = pltpu.make_async_remote_copy(
            src_ref=own,
            dst_ref=near_ref.at[hop, sector],
            send_sem=send_sem.at[number],
            recv_sem=recv_sem.at[number],
            device_id=(lax.rem(sector + flip, 2), lax.rem(slab + hop, SLABS)),
            device_id_type=MESH,
        )
        copy.start()
        copies.append(copy)
    for copy in copies:
        copy.wait()
    basis_copy.wait()


def gather_near(mode_basis, mode_coeff, *lists):
    vmem = pl.BlockSpec(memory_space=pltpu.VMEM)
    values = [mode_basis, mode_coeff] + [one.reshape(1, SLOTS) for one in lists]
    return pl.pallas_call(
        gather_kernel,
        out_shape=[
            jax.ShapeDtypeStruct((3, 2, SLOTS + 8, 128), F32),
            jax.ShapeDtypeStruct((MODES, (LAST - FIRST) * TILE), BF16),
        ],
        in_specs=[pl.BlockSpec(memory_space=pltpu.HBM)] * 6,
        out_specs=[vmem, vmem],
        scratch_shapes=[
            pltpu.VMEM((SLOTS, MODES), BF16),
            pltpu.VMEM((1, SLOTS), BF16),
            pltpu.VMEM((1, SLOTS), jnp.int32),
            pltpu.VMEM((1, SLOTS), jnp.int32),
            pltpu.VMEM((1, SLOTS), jnp.int32),
            pltpu.VMEM((SLOTS + 8, 128), F32),
            pltpu.SemaphoreType.DMA,
            pltpu.SemaphoreType.DMA((5,)),
            pltpu.SemaphoreType.DMA((5,)),
            pltpu.SemaphoreType.DMA((5,)),
        ],
        compiler_params=pltpu.CompilerParams(
            collective_id=0, has_side_effects=True, vmem_limit_bytes=20 << 20
        ),
        name="gather_near",
    )(*(pltpu.with_memory_space_constraint(value, pltpu.HBM) for value in values))


def circle(phase):
    turns = phase * (0.5 / math.pi)
    part = turns - jnp.round(turns)
    square = part * part
    sine = SIN_TERMS[-1]
    for term in SIN_TERMS[-2::-1]:
        sine = sine * square + term
    sine = sine * part
    cosine = COS_TERMS[-1]
    for term in COS_TERMS[-2::-1]:
        cosine = cosine * square + term
    double = sine + sine
    return 1.0 - double * sine, double * cosine


TOGETHER = 28
STEPS_EACH = (LAST - FIRST) // 2 // TOGETHER
LISTED = NEAR // STEPS_EACH
TASKS = 4


def render_kernel(
    near, basis, canvas, left, right, marks, slots, table, tasks, slots_sem, table_sem
):
    sector = lax.axis_index("sector")
    slab = lax.axis_index("slab")
    base_row = 2 * LINES * slab + LINES * sector
    slots_copy = pltpu.make_async_copy(near.at[:, :, pl.ds(SLOTS, 8)], slots, slots_sem)
    slots_copy.start()
    for hop in range(3):
        for side in range(2):
            tile_row, column, live = (
                near[hop, side, SLOTS + number : SLOTS + number + 1, :].astype(jnp.int32)
                for number in (1, 2, 3)
            )
            top = base_row - tile_row
            at = 2 * hop + side
            marks[at, 0:1, :] = top
            marks[at, 1:2, :] = column >> 7
            marks[at, 2:3, :] = column & 127
            for part in range(2):
                start = top + part * HALF
                reaches = (start >= 17 - (HALF - 1)) & (start <= 238) & (live > 0)
                marks[at, 3 + part : 4 + part, :] = reaches.astype(jnp.int32)
    table_copy = pltpu.make_async_copy(marks, table, table_sem)
    table_copy.start()
    canvas[...] = jnp.zeros_like(canvas)
    coeff = [
        jnp.concatenate([near[hop, side, :SLOTS, :MODES] for side in range(2)], axis=0).astype(BF16)
        for hop in range(3)
    ]

    def form(part, step):
        mix = jnp.concatenate([coeff[2 * part], coeff[1]], axis=0)
        row = (part * STEPS_EACH + step) * TOGETHER
        columns = pl.ds(pl.multiple_of(row * TILE, TOGETHER * TILE), TOGETHER * TILE)
        phases = dot(mix, basis[:, columns])
        for extra in range(TOGETHER):
            place = pl.ds(pl.multiple_of((row + extra + FIRST + PAD) * WIDE, 8), 64)
            at = extra * TILE
            left[place, :] = phases[:, at : at + 128]
            right[place, :] = phases[:, at + 128 : at + 256]

    @pl.loop(0, STEPS_EACH)
    def _(step):
        form(0, step)

    table_copy.wait()
    slots_copy.wait()

    def form_and_list(step, count):
        form(1, step)
        for extra in range(LISTED):
            slot = step * LISTED + extra
            for part in range(2):
                tasks[count] = 2 * slot + part
                count = count + table[slot >> 4, 3 + part, slot & 15]
        return count

    count = lax.fori_loop(0, STEPS_EACH, form_and_list, 0)
    lane = lax.broadcasted_iota(jnp.int32, (1, 128), 1)
    down = lax.broadcasted_iota(jnp.int32, (HALF, 1), 0)
    reach = 7 * (TILE - 2)

    def tile_part(number):
        task = tasks[jnp.minimum(number, count - 1)]
        slot = task >> 1
        part = task & 1
        group = slot >> 4
        at = slot & 15
        weight = jnp.where(number < count, slots[slot >> 5, group & 1, 0, at], 0.0)
        top = table[group, 0, at] + part * HALF
        block = table[group, 1, at]
        shift = table[group, 2, at]
        start = (top + PAD) * WIDE + (slot & 63)
        vertical = jnp.abs(2 * (top + down) - (TILE - 1))
        vertical = jnp.where(8 * vertical <= reach, 4 * vertical, 4 * reach)
        vertical = jnp.broadcast_to(vertical, (HALF, 128))
        place = (lane - shift) & 127
        room_left = reach - 7 * ((TILE - 1) - 2 * place)
        room_right = reach - 7 * (2 * place + 1)
        both = []
        for ref, room in ((left, room_left), (right, room_right)):
            wave = pltpu.roll(ref[pl.ds(start, HALF, stride=WIDE), :], shift, 1)
            inside = vertical <= room
            amplitude = jnp.where(inside, weight, 0.0)
            cosine, sine = circle(jnp.where(inside, wave, 0.0))
            both.append((cosine * amplitude, sine * amplitude))
        rows = pl.ds(pl.multiple_of(part * HALF, HALF), HALF)
        return block, rows, jnp.broadcast_to(lane >= shift, (HALF, 128)), both

    def deposit(block, rows, kept, both):
        for comp in range(2):
            one, two = both[0][comp], both[1][comp]
            at = comp * BLOCKS + block
            past = jnp.minimum(at + 2, 2 * BLOCKS - 1)
            canvas[at, rows, :] += jnp.where(kept, one, 0.0)
            canvas[at + 1, rows, :] += jnp.where(kept, two, one)
            canvas[past, rows, :] += jnp.where(kept, 0.0, two)

    @pl.loop(0, (count + TASKS - 1) // TASKS)
    def _(step):
        before = None
        for extra in range(TASKS):
            piece = tile_part(TASKS * step + extra)
            if before is not None:
                deposit(*before)
            before = piece
        deposit(*before)


def render(near, mode_basis):
    vmem = pl.BlockSpec(memory_space=pltpu.VMEM)
    return pl.pallas_call(
        render_kernel,
        out_shape=jax.ShapeDtypeStruct((2 * BLOCKS, WIDE, 128), F32),
        in_specs=[vmem, vmem],
        out_specs=vmem,
        scratch_shapes=[
            pltpu.VMEM(((TILE + 2 * PAD) * WIDE, 128), F32),
            pltpu.VMEM(((TILE + 2 * PAD) * WIDE, 128), F32),
            pltpu.VMEM((6, 8, 128), jnp.int32),
            pltpu.SMEM((3, 2, 8, 128), F32),
            pltpu.SMEM((6, 8, 128), jnp.int32),
            pltpu.SMEM((2 * NEAR + 8,), jnp.int32),
            pltpu.SemaphoreType.DMA,
            pltpu.SemaphoreType.DMA,
        ],
        compiler_params=pltpu.CompilerParams(vmem_limit_bytes=40 << 20),
        name="render_rows",
    )(near, mode_basis)


def encode(value):
    size = jnp.log(jnp.abs(value)) * (STEPS / math.log(2.0)) + (LOW * STEPS + 0.5)
    code = jnp.maximum(size, 0.0).astype(jnp.int32)
    return jnp.where(value < 0.0, -code, code)


def decode(code):
    size = jnp.abs(code).astype(F32) * (math.log(2.0) / STEPS) - LOW * math.log(2.0)
    value = jnp.exp(size)
    return jnp.where(code == 0, 0.0, jnp.where(code < 0, -value, value))


def exchange_kernel(
    field, turn, twist, long_turn, mid_ref, wide, outbox, inbox, plain, send_sem, recv_sem
):
    sector = lax.axis_index("sector")
    slab = lax.axis_index("slab")
    me = sector * SLABS + slab
    source = 2 * slab + sector
    barrier = pltpu.get_barrier_semaphore()

    @pl.loop(1, DEVICES)
    def _(step):
        other = (me + step) & (DEVICES - 1)
        pl.semaphore_signal(
            barrier, inc=1, device_id=(other >> 6, other & (SLABS - 1)), device_id_type=MESH
        )

    lines = field.reshape(2 * BLOCKS * WIDE, 128)
    codes = wide.reshape(DEVICES * SHORT, 128)
    values = plain.reshape(DEVICES * SHORT, 128)
    for chunk in range(CHUNKS):

        @pl.loop(0, CHUNK // 4)
        def _(step):
            parts = []
            for pair in range(2):
                line = chunk * CHUNK + 4 * step + 2 * pair
                both = [lines[pl.ds(line + e, 2 * BLOCKS, stride=WIDE), :] for e in range(2)]
                mid = dot_short(turn[...], jnp.concatenate(both, axis=1))
                for e in range(2):
                    real = mid[:64, 128 * e : 128 * e + 128]
                    imag = mid[64:, 128 * e : 128 * e + 128]
                    turned_real = real * twist[0] + imag * twist[1]
                    turned_imag = imag * twist[0] - real * twist[1]
                    parts.append(jnp.concatenate([turned_real, turned_imag], axis=1))
            done = encode(dot_long(jnp.concatenate(parts, axis=0), long_turn))
            for e in range(4):
                some = done[64 * e : 64 * e + 64]
                some = jnp.concatenate([some[:, :128], some[:, 128:]], axis=0).T
                codes[pl.ds(4 * step + e, DEVICES, stride=SHORT), :] = some

        @pl.loop(0, DEVICES // 16)
        def _(step):
            some = pl.ds(step * 16, 16)
            outbox[chunk, some] = wide[some, :CHUNK].astype(jnp.int16)

        if chunk == 0:
            pl.semaphore_wait(barrier, DEVICES - 1)

        @pl.loop(1, DEVICES)
        def _(step):
            other = (me + step) & (DEVICES - 1)
            pltpu.make_async_remote_copy(
                src_ref=outbox.at[chunk, other],
                dst_ref=inbox.at[chunk, source],
                send_sem=send_sem.at[chunk],
                recv_sem=recv_sem.at[chunk],
                device_id=(other >> 6, other & (SLABS - 1)),
                device_id_type=MESH,
            ).start()

        inbox[chunk, source] = outbox[chunk, me]

    for chunk in range(CHUNKS):
        most = inbox.at[chunk, pl.ds(0, DEVICES - 1)]
        pltpu.make_async_copy(most, most, recv_sem.at[chunk]).wait()

        @pl.loop(0, DEVICES // 16)
        def _(step):
            some = pl.ds(step * 16, 16)
            plain[some, :CHUNK] = decode(inbox[chunk, some].astype(jnp.int32))

        @pl.loop(0, CHUNK // 4)
        def _(step):
            parts = []
            for e in range(4):
                turned = values[pl.ds(4 * step + e, DEVICES, stride=SHORT), :].T
                parts.append(jnp.concatenate([turned[:64], turned[64:]], axis=1))
            mid = dot_long(jnp.concatenate(parts, axis=0), long_turn)
            for e in range(4):
                line = chunk * CHUNK + 4 * step + e
                cos = twist[0, pl.ds(line, 1), :]
                sin = twist[1, pl.ds(line, 1), :]
                real = mid[64 * e : 64 * e + 64, :128]
                imag = mid[64 * e : 64 * e + 64, 128:]
                mid_ref[0, line, :LINES] = real * cos + imag * sin
                mid_ref[1, line, :LINES] = imag * cos - real * sin

    for chunk in range(CHUNKS):
        most = outbox.at[chunk, pl.ds(0, DEVICES - 1)]
        pltpu.make_async_copy(most, most, send_sem.at[chunk]).wait()


def exchange(field, *consts):
    vmem = pl.BlockSpec(memory_space=pltpu.VMEM)
    return pl.pallas_call(
        exchange_kernel,
        out_shape=jax.ShapeDtypeStruct((2, LINES, WIDE, 128), F32),
        in_specs=[vmem] * 4,
        out_specs=vmem,
        scratch_shapes=[
            pltpu.VMEM((DEVICES, SHORT, 128), jnp.int32),
            pltpu.VMEM((CHUNKS, DEVICES, CHUNK, 128), jnp.int16),
            pltpu.VMEM((CHUNKS, DEVICES, CHUNK, 128), jnp.int16),
            pltpu.VMEM((DEVICES, SHORT, 128), F32),
            pltpu.SemaphoreType.DMA((CHUNKS,)),
            pltpu.SemaphoreType.DMA((CHUNKS,)),
        ],
        compiler_params=pltpu.CompilerParams(
            collective_id=1, has_side_effects=True, vmem_limit_bytes=32 << 20
        ),
        name="exchange",
    )(field, *consts)


def finish_kernel(mid_ref, turn, out_hbm, turned, ready, out_sem):
    lines = mid_ref.reshape(2 * LINES * WIDE, 128)

    def leave(group):
        rows = pl.ds(group * 8, 8)
        return pltpu.make_async_copy(ready.at[:, rows], out_hbm.at[:, rows], out_sem.at[group])

    for group in range(LINES // 8):
        for pair in range(4):
            line = group * 8 + 2 * pair
            both = [lines[pl.ds(line + e, 2 * LINES, stride=WIDE), :] for e in range(2)]
            done = dot_short(turn[...], jnp.concatenate(both, axis=1))
            for e in range(2):
                turned[group % 2, pl.ds(2 * pair + e, 2 * LINES, stride=8), :] = done[
                    :, 128 * e : 128 * e + 128
                ]
        for comp in range(2):
            for block in range(LINES):
                at = (comp * LINES + block) * 8
                ready[comp, 8 * group : 8 * group + 8, 128 * block : 128 * block + 128] = turned[
                    group % 2, at : at + 8, :
                ]
        leave(group).start()
    for group in range(LINES // 8):
        leave(group).wait()


def finish(mid, turn):
    vmem = pl.BlockSpec(memory_space=pltpu.VMEM)
    return pl.pallas_call(
        finish_kernel,
        out_shape=jax.ShapeDtypeStruct((2, LINES, GRID), F32),
        in_specs=[vmem, vmem],
        out_specs=pl.BlockSpec(memory_space=pl.ANY),
        scratch_shapes=[
            pltpu.VMEM((2, 2 * LINES * 8, 128), F32),
            pltpu.VMEM((2, LINES, GRID), F32),
            pltpu.SemaphoreType.DMA((LINES // 8,)),
        ],
        compiler_params=pltpu.CompilerParams(vmem_limit_bytes=24 << 20),
        name="finish",
    )(mid, turn)


def body(mode_basis, mode_coeff, reflect, tile_row, tile_col, slot_live):
    turn, twist, long_turn, last_turn = (jnp.asarray(table) for table in tables())
    near, basis = gather_near(mode_basis, mode_coeff, reflect, tile_row, tile_col, slot_live)
    field = render(near, basis)
    mid = exchange(field, turn, twist, long_turn)
    return finish(mid, last_turn)


def solution(mesh):
    placed = (
        P(),
        P(("sector", "slab"), None),
        P(("sector", "slab")),
        P(("sector", "slab")),
        P(("sector", "slab")),
        P(("sector", "slab")),
    )
    return jax.shard_map(
        body,
        mesh=mesh,
        in_specs=placed,
        out_specs=P(None, ("sector", "slab"), None),
        check_vma=False,
    )
```

```python
import functools
import math

import jax
import jax.numpy as jnp
import ml_dtypes
import numpy as np
from jax import lax
from jax.experimental import pallas as pl
from jax.experimental.pallas import tpu as pltpu
from jax.sharding import PartitionSpec as P

GRID = 8192
TILE = 256
SLOTS = 16
MODES = 64
SLABS = 64
DEVICES = 128
LINES = GRID // DEVICES
BLOCKS = GRID // 128
NEAR = 6 * SLOTS
CHUNK = 16
CHUNKS = LINES // CHUNK
PAD = 16
HALF = 32
FIRST, LAST = 16, 240
WIDE = LINES + 8
SHORT = CHUNK + 8
MESH = pl.DeviceIdType.MESH
F32 = jnp.float32
BF16 = jnp.bfloat16

LOW = 12.0
STEPS = 32766.0 / (LOW + 15.25)


def polynomial(values, powers):
    spots = np.cos(np.pi * (np.arange(400) + 0.5) / 800) * 0.5
    table = np.stack([spots**power for power in powers], axis=1)
    return [float(c) for c in np.linalg.lstsq(table, values(np.pi * spots), rcond=None)[0]]


SIN_TERMS = polynomial(np.sin, (1, 3, 5, 7))
COS_TERMS = polynomial(np.cos, (0, 2, 4, 6))


def halves(table):
    high = table.astype(ml_dtypes.bfloat16)
    low = (table - high.astype(np.float64)).astype(ml_dtypes.bfloat16)
    return high, low


def angles(left, right, total):
    turns = np.outer(np.arange(left), np.arange(right)) % total
    return 2.0 * math.pi * turns / total


def stacked(table):
    high, low = halves(table)
    return np.block([[high, high], [low, np.zeros_like(low)]])


def tables():
    first = angles(64, 64, 64)
    turn = np.block([[np.cos(first), np.sin(first)], [-np.sin(first), np.cos(first)]])
    twist = angles(64, 128, GRID)
    second = angles(128, 128, 128)
    long_turn = np.block([[np.cos(second), -np.sin(second)], [np.sin(second), np.cos(second)]])
    return (
        stacked(turn),
        np.stack([np.cos(twist), np.sin(twist)]).astype(np.float32),
        np.stack(halves(long_turn)),
        stacked(turn / GRID),
    )


def split(value):
    high = value.astype(BF16)
    return high, (value - high.astype(F32)).astype(BF16)


def dot(left, right):
    return jnp.dot(left, right, preferred_element_type=F32)


def dot_short(table, value):
    high, low = split(value)
    both = dot(table, jnp.concatenate([high, low], axis=0))
    return both[:128] + both[128:]


def dot_long(value, tables):
    high, low = split(value)
    return dot(high, tables[0]) + dot(high, tables[1]) + dot(low, tables[0])


def gather_kernel(
    basis_hbm,
    coeff_hbm,
    reflect_hbm,
    row_hbm,
    column_hbm,
    live_hbm,
    near_ref,
    basis_ref,
    coeff_ref,
    reflect_ref,
    row_ref,
    column_ref,
    live_ref,
    own,
    basis_sem,
    in_sem,
    send_sem,
    recv_sem,
):
    sector = lax.axis_index("sector")
    slab = lax.axis_index("slab")
    barrier = pltpu.get_barrier_semaphore()
    used = pl.ds(FIRST * TILE, (LAST - FIRST) * TILE)
    basis_copy = pltpu.make_async_copy(basis_hbm.at[:, used], basis_ref, basis_sem)
    sources = (coeff_hbm, reflect_hbm, row_hbm, column_hbm, live_hbm)
    held = (coeff_ref, reflect_ref, row_ref, column_ref, live_ref)
    loads = [
        pltpu.make_async_copy(one, two, in_sem.at[number])
        for number, (one, two) in enumerate(zip(sources, held))
    ]
    for load in loads:
        load.start()
    basis_copy.start()
    others = [(flip, hop) for hop in range(3) for flip in range(2)][1:]
    for flip, hop in others:
        for step in {hop, -hop}:
            pl.semaphore_signal(
                barrier,
                inc=1,
                device_id=(lax.rem(sector + flip, 2), lax.rem(slab + step + SLABS, SLABS)),
                device_id_type=MESH,
            )
    for load in loads:
        load.wait()
    own[:SLOTS, :MODES] = coeff_ref[...].astype(F32)
    for number, ref in enumerate((reflect_ref, row_ref, column_ref, live_ref)):
        own[SLOTS + number : SLOTS + number + 1, :SLOTS] = ref[...].astype(F32)
    near_ref[0, sector] = own[...]
    pl.semaphore_wait(barrier, 9)
    copies = []
    for number, (flip, hop) in enumerate(others):
        copy = pltpu.make_async_remote_copy(
            src_ref=own,
            dst_ref=near_ref.at[hop, sector],
            send_sem=send_sem.at[number],
            recv_sem=recv_sem.at[number],
            device_id=(lax.rem(sector + flip, 2), lax.rem(slab + hop, SLABS)),
            device_id_type=MESH,
        )
        copy.start()
        copies.append(copy)
    for copy in copies:
        copy.wait()
    basis_copy.wait()


def gather_near(mode_basis, mode_coeff, *lists):
    vmem = pl.BlockSpec(memory_space=pltpu.VMEM)
    values = [mode_basis, mode_coeff] + [one.reshape(1, SLOTS) for one in lists]
    return pl.pallas_call(
        gather_kernel,
        out_shape=[
            jax.ShapeDtypeStruct((3, 2, SLOTS + 8, 128), F32),
            jax.ShapeDtypeStruct((MODES, (LAST - FIRST) * TILE), BF16),
        ],
        in_specs=[pl.BlockSpec(memory_space=pltpu.HBM)] * 6,
        out_specs=[vmem, vmem],
        scratch_shapes=[
            pltpu.VMEM((SLOTS, MODES), BF16),
            pltpu.VMEM((1, SLOTS), BF16),
            pltpu.VMEM((1, SLOTS), jnp.int32),
            pltpu.VMEM((1, SLOTS), jnp.int32),
            pltpu.VMEM((1, SLOTS), jnp.int32),
            pltpu.VMEM((SLOTS + 8, 128), F32),
            pltpu.SemaphoreType.DMA,
            pltpu.SemaphoreType.DMA((5,)),
            pltpu.SemaphoreType.DMA((5,)),
            pltpu.SemaphoreType.DMA((5,)),
        ],
        compiler_params=pltpu.CompilerParams(
            collective_id=0, has_side_effects=True, vmem_limit_bytes=20 << 20
        ),
        name="gather_near",
    )(*(pltpu.with_memory_space_constraint(value, pltpu.HBM) for value in values))


def circle(phase):
    turns = phase * (0.5 / math.pi)
    part = turns - jnp.round(turns)
    square = part * part
    sine = SIN_TERMS[-1]
    for term in SIN_TERMS[-2::-1]:
        sine = sine * square + term
    sine = sine * part
    cosine = COS_TERMS[-1]
    for term in COS_TERMS[-2::-1]:
        cosine = cosine * square + term
    double = sine + sine
    return 1.0 - double * sine, double * cosine


TOGETHER = 28
STEPS_EACH = (LAST - FIRST) // 2 // TOGETHER
LISTED = NEAR // STEPS_EACH
TASKS = 4


def render_kernel(
    near, basis, canvas, left, right, marks, slots, table, tasks, slots_sem, table_sem
):
    sector = lax.axis_index("sector")
    slab = lax.axis_index("slab")
    base_row = 2 * LINES * slab + LINES * sector
    slots_copy = pltpu.make_async_copy(near.at[:, :, pl.ds(SLOTS, 8)], slots, slots_sem)
    slots_copy.start()
    for hop in range(3):
        for side in range(2):
            tile_row, column, live = (
                near[hop, side, SLOTS + number : SLOTS + number + 1, :].astype(jnp.int32)
                for number in (1, 2, 3)
            )
            top = base_row - tile_row
            at = 2 * hop + side
            marks[at, 0:1, :] = top
            marks[at, 1:2, :] = column >> 7
            marks[at, 2:3, :] = column & 127
            for part in range(2):
                start = top + part * HALF
                reaches = (start >= 17 - (HALF - 1)) & (start <= 238) & (live > 0)
                marks[at, 3 + part : 4 + part, :] = reaches.astype(jnp.int32)
    table_copy = pltpu.make_async_copy(marks, table, table_sem)
    table_copy.start()
    canvas[...] = jnp.zeros_like(canvas)
    coeff = [
        jnp.concatenate([near[hop, side, :SLOTS, :MODES] for side in range(2)], axis=0).astype(BF16)
        for hop in range(3)
    ]

    def form(part, step):
        mix = jnp.concatenate([coeff[2 * part], coeff[1]], axis=0)
        row = (part * STEPS_EACH + step) * TOGETHER
        columns = pl.ds(pl.multiple_of(row * TILE, TOGETHER * TILE), TOGETHER * TILE)
        phases = dot(mix, basis[:, columns])
        for extra in range(TOGETHER):
            place = pl.ds(pl.multiple_of((row + extra + FIRST + PAD) * WIDE, 8), 64)
            at = extra * TILE
            left[place, :] = phases[:, at : at + 128]
            right[place, :] = phases[:, at + 128 : at + 256]

    @pl.loop(0, STEPS_EACH)
    def _(step):
        form(0, step)

    table_copy.wait()
    slots_copy.wait()

    def form_and_list(step, count):
        form(1, step)
        for extra in range(LISTED):
            slot = step * LISTED + extra
            for part in range(2):
                tasks[count] = 2 * slot + part
                count = count + table[slot >> 4, 3 + part, slot & 15]
        return count

    count = lax.fori_loop(0, STEPS_EACH, form_and_list, 0)
    lane = lax.broadcasted_iota(jnp.int32, (1, 128), 1)
    down = lax.broadcasted_iota(jnp.int32, (HALF, 1), 0)
    reach = 7 * (TILE - 2)

    def tile_part(number):
        task = tasks[jnp.minimum(number, count - 1)]
        slot = task >> 1
        part = task & 1
        group = slot >> 4
        at = slot & 15
        weight = jnp.where(number < count, slots[slot >> 5, group & 1, 0, at], 0.0)
        top = table[group, 0, at] + part * HALF
        block = table[group, 1, at]
        shift = table[group, 2, at]
        start = (top + PAD) * WIDE + (slot & 63)
        vertical = jnp.abs(2 * (top + down) - (TILE - 1))
        vertical = jnp.where(8 * vertical <= reach, 4 * vertical, 4 * reach)
        vertical = jnp.broadcast_to(vertical, (HALF, 128))
        place = (lane - shift) & 127
        room_left = reach - 7 * ((TILE - 1) - 2 * place)
        room_right = reach - 7 * (2 * place + 1)
        both = []
        for ref, room in ((left, room_left), (right, room_right)):
            wave = pltpu.roll(ref[pl.ds(start, HALF, stride=WIDE), :], shift, 1)
            inside = vertical <= room
            amplitude = jnp.where(inside, weight, 0.0)
            cosine, sine = circle(jnp.where(inside, wave, 0.0))
            both.append((cosine * amplitude, sine * amplitude))
        rows = pl.ds(pl.multiple_of(part * HALF, HALF), HALF)
        return block, rows, jnp.broadcast_to(lane >= shift, (HALF, 128)), both

    def deposit(block, rows, kept, both):
        for comp in range(2):
            one, two = both[0][comp], both[1][comp]
            at = comp * BLOCKS + block
            past = jnp.minimum(at + 2, 2 * BLOCKS - 1)
            canvas[at, rows, :] += jnp.where(kept, one, 0.0)
            canvas[at + 1, rows, :] += jnp.where(kept, two, one)
            canvas[past, rows, :] += jnp.where(kept, 0.0, two)

    @pl.loop(0, (count + TASKS - 1) // TASKS)
    def _(step):
        before = None
        for extra in range(TASKS):
            piece = tile_part(TASKS * step + extra)
            if before is not None:
                deposit(*before)
            before = piece
        deposit(*before)


def render(near, mode_basis):
    vmem = pl.BlockSpec(memory_space=pltpu.VMEM)
    return pl.pallas_call(
        render_kernel,
        out_shape=jax.ShapeDtypeStruct((2 * BLOCKS, WIDE, 128), F32),
        in_specs=[vmem, vmem],
        out_specs=vmem,
        scratch_shapes=[
            pltpu.VMEM(((TILE + 2 * PAD) * WIDE, 128), F32),
            pltpu.VMEM(((TILE + 2 * PAD) * WIDE, 128), F32),
            pltpu.VMEM((6, 8, 128), jnp.int32),
            pltpu.SMEM((3, 2, 8, 128), F32),
            pltpu.SMEM((6, 8, 128), jnp.int32),
            pltpu.SMEM((2 * NEAR + 8,), jnp.int32),
            pltpu.SemaphoreType.DMA,
            pltpu.SemaphoreType.DMA,
        ],
        compiler_params=pltpu.CompilerParams(vmem_limit_bytes=40 << 20),
        name="render_rows",
    )(near, mode_basis)


def encode(value):
    size = jnp.log(jnp.abs(value)) * (STEPS / math.log(2.0)) + (LOW * STEPS + 0.5)
    code = jnp.maximum(size, 0.0).astype(jnp.int32)
    return jnp.where(value < 0.0, -code, code)


def decode(code):
    size = jnp.abs(code).astype(F32) * (math.log(2.0) / STEPS) - LOW * math.log(2.0)
    value = jnp.exp(size)
    return jnp.where(code == 0, 0.0, jnp.where(code < 0, -value, value))


def exchange_kernel(
    field,
    turn,
    twist,
    long_turn,
    mid_ref,
    wide,
    box,
    handed,
    early,
    inbox,
    plain,
    send_sem,
    recv_sem,
    swap_send_sem,
    swap_recv_sem,
):
    sector = lax.axis_index("sector")
    slab = lax.axis_index("slab")
    other_sector = 1 - sector
    barrier = pltpu.get_barrier_semaphore()

    def greet(target):
        pl.semaphore_signal(barrier, inc=1, device_id=target, device_id_type=MESH)

    greet((other_sector, slab))

    @pl.loop(1, SLABS, unroll=9)
    def _(step):
        greet((sector, (slab + step) & (SLABS - 1)))

    def swap(chunk):
        return pltpu.make_async_remote_copy(
            src_ref=early.at[:, other_sector] if chunk == 0 else handed.at[chunk - 1],
            dst_ref=(inbox if chunk == 0 else box).at[chunk, :, sector],
            send_sem=swap_send_sem.at[chunk],
            recv_sem=swap_recv_sem.at[chunk],
            device_id=(other_sector, slab),
            device_id_type=MESH,
        )

    lines = field.reshape(2 * BLOCKS * WIDE, 128)
    codes = wide.reshape(DEVICES * SHORT, 128)
    values = plain.reshape(DEVICES * SHORT, 128)
    for chunk in range(CHUNKS):

        @pl.loop(0, CHUNK // 4)
        def _(step):
            parts = []
            for pair in range(2):
                line = chunk * CHUNK + 4 * step + 2 * pair
                both = [lines[pl.ds(line + e, 2 * BLOCKS, stride=WIDE), :] for e in range(2)]
                mid = dot_short(turn[...], jnp.concatenate(both, axis=1))
                for e in range(2):
                    real = mid[:64, 128 * e : 128 * e + 128]
                    imag = mid[64:, 128 * e : 128 * e + 128]
                    turned_real = real * twist[0] + imag * twist[1]
                    turned_imag = imag * twist[0] - real * twist[1]
                    parts.append(jnp.concatenate([turned_real, turned_imag], axis=1))
            done = encode(dot_long(jnp.concatenate(parts, axis=0), long_turn))
            for e in range(4):
                some = done[64 * e : 64 * e + 64]
                some = jnp.concatenate([some[:, :128], some[:, 128:]], axis=0).T
                codes[pl.ds(4 * step + e, DEVICES, stride=SHORT), :] = some

        @pl.loop(0, SLABS // 16)
        def _(step):
            some = pl.ds(step * 16, 16)
            for side, to in ((sector, sector), (other_sector, other_sector)):
                packed = wide[pl.ds(to * SLABS + step * 16, 16), :CHUNK].astype(jnp.int16)
                if chunk > 0 and side is other_sector:
                    handed[chunk - 1, some] = packed
                else:
                    box[chunk, some, side] = packed

        if chunk == 0:
            pl.semaphore_wait(barrier, SLABS)
        else:
            swap(chunk).start()
            swap(chunk).wait()
        land = early if chunk == 0 else inbox.at[chunk]

        @pl.loop(1, SLABS, unroll=3)
        def _(step):
            target = (slab + step) & (SLABS - 1)
            pltpu.make_async_remote_copy(
                src_ref=box.at[chunk, target],
                dst_ref=land.at[slab],
                send_sem=send_sem.at[chunk],
                recv_sem=recv_sem.at[chunk],
                device_id=(sector, target),
                device_id_type=MESH,
            ).start()

        land[slab] = box[chunk, slab]

    for chunk in range(CHUNKS):
        most = (early if chunk == 0 else inbox.at[chunk]).at[pl.ds(0, SLABS - 1)]
        pltpu.make_async_copy(most, most, recv_sem.at[chunk]).wait()
        if chunk == 0:
            swap(0).start()
            inbox[0, :, sector] = early[:, sector]
            swap(0).wait()

        @pl.loop(0, DEVICES // 16)
        def _(step):
            codes_in = inbox[chunk, pl.ds(step * 8, 8)].astype(jnp.int32)
            plain[pl.ds(step * 16, 16), :CHUNK] = decode(codes_in).reshape(16, CHUNK, 128)

        @pl.loop(0, CHUNK // 4)
        def _(step):
            parts = []
            for e in range(4):
                turned = values[pl.ds(4 * step + e, DEVICES, stride=SHORT), :].T
                parts.append(jnp.concatenate([turned[:64], turned[64:]], axis=1))
            mid = dot_long(jnp.concatenate(parts, axis=0), long_turn)
            for e in range(4):
                line = chunk * CHUNK + 4 * step + e
                cos = twist[0, pl.ds(line, 1), :]
                sin = twist[1, pl.ds(line, 1), :]
                real = mid[64 * e : 64 * e + 64, :128]
                imag = mid[64 * e : 64 * e + 64, 128:]
                mid_ref[0, line, :LINES] = real * cos + imag * sin
                mid_ref[1, line, :LINES] = imag * cos - real * sin

    for chunk in range(CHUNKS):
        most = box.at[chunk, pl.ds(0, SLABS - 1)]
        pltpu.make_async_copy(most, most, send_sem.at[chunk]).wait()


def exchange(field, *consts):
    vmem = pl.BlockSpec(memory_space=pltpu.VMEM)
    return pl.pallas_call(
        exchange_kernel,
        out_shape=jax.ShapeDtypeStruct((2, LINES, WIDE, 128), F32),
        in_specs=[vmem] * 4,
        out_specs=vmem,
        scratch_shapes=[
            pltpu.VMEM((DEVICES, SHORT, 128), jnp.int32),
            pltpu.VMEM((CHUNKS, SLABS, 2, CHUNK, 128), jnp.int16),
            pltpu.VMEM((CHUNKS - 1, SLABS, CHUNK, 128), jnp.int16),
            pltpu.VMEM((SLABS, 2, CHUNK, 128), jnp.int16),
            pltpu.VMEM((CHUNKS, SLABS, 2, CHUNK, 128), jnp.int16),
            pltpu.VMEM((DEVICES, SHORT, 128), F32),
            pltpu.SemaphoreType.DMA((CHUNKS,)),
            pltpu.SemaphoreType.DMA((CHUNKS,)),
            pltpu.SemaphoreType.DMA((CHUNKS,)),
            pltpu.SemaphoreType.DMA((CHUNKS,)),
        ],
        compiler_params=pltpu.CompilerParams(
            collective_id=1, has_side_effects=True, vmem_limit_bytes=32 << 20
        ),
        name="exchange",
    )(field, *consts)


def finish_kernel(mid_ref, turn, out_hbm, turned, ready, out_sem):
    lines = mid_ref.reshape(2 * LINES * WIDE, 128)

    def leave(group):
        rows = pl.ds(group * 8, 8)
        return pltpu.make_async_copy(ready.at[:, rows], out_hbm.at[:, rows], out_sem.at[group])

    for group in range(LINES // 8):
        for pair in range(4):
            line = group * 8 + 2 * pair
            both = [lines[pl.ds(line + e, 2 * LINES, stride=WIDE), :] for e in range(2)]
            done = dot_short(turn[...], jnp.concatenate(both, axis=1))
            for e in range(2):
                turned[group % 2, pl.ds(2 * pair + e, 2 * LINES, stride=8), :] = done[
                    :, 128 * e : 128 * e + 128
                ]
        for comp in range(2):
            for block in range(LINES):
                at = (comp * LINES + block) * 8
                ready[comp, 8 * group : 8 * group + 8, 128 * block : 128 * block + 128] = turned[
                    group % 2, at : at + 8, :
                ]
        leave(group).start()
    for group in range(LINES // 8):
        leave(group).wait()


def finish(mid, turn):
    vmem = pl.BlockSpec(memory_space=pltpu.VMEM)
    return pl.pallas_call(
        finish_kernel,
        out_shape=jax.ShapeDtypeStruct((2, LINES, GRID), F32),
        in_specs=[vmem, vmem],
        out_specs=pl.BlockSpec(memory_space=pl.ANY),
        scratch_shapes=[
            pltpu.VMEM((2, 2 * LINES * 8, 128), F32),
            pltpu.VMEM((2, LINES, GRID), F32),
            pltpu.SemaphoreType.DMA((LINES // 8,)),
        ],
        compiler_params=pltpu.CompilerParams(vmem_limit_bytes=24 << 20),
        name="finish",
    )(mid, turn)


def body(mode_basis, mode_coeff, reflect, tile_row, tile_col, slot_live):
    turn, twist, long_turn, last_turn = (jnp.asarray(table) for table in tables())
    near, basis = gather_near(mode_basis, mode_coeff, reflect, tile_row, tile_col, slot_live)
    field = render(near, basis)
    mid = exchange(field, turn, twist, long_turn)
    return finish(mid, last_turn)


def solution(mesh):
    placed = (
        P(),
        P(("sector", "slab"), None),
        P(("sector", "slab")),
        P(("sector", "slab")),
        P(("sector", "slab")),
        P(("sector", "slab")),
    )
    return jax.shard_map(
        body,
        mesh=mesh,
        in_specs=placed,
        out_specs=P(None, ("sector", "slab"), None),
        check_vma=False,
    )
```

```python
import functools
import math

import jax
import jax.numpy as jnp
import ml_dtypes
import numpy as np
from jax import lax
from jax.experimental import pallas as pl
from jax.experimental.pallas import tpu as pltpu
from jax.sharding import PartitionSpec as P

GRID = 8192
TILE = 256
SLOTS = 16
MODES = 64
SLABS = 64
DEVICES = 128
LINES = GRID // DEVICES
BLOCKS = GRID // 128
NEAR = 6 * SLOTS
CHUNK = 16
CHUNKS = LINES // CHUNK
PAD = 16
HALF = 32
FIRST, LAST = 16, 240
WIDE = LINES + 8
SHORT = CHUNK + 8
MESH = pl.DeviceIdType.MESH
F32 = jnp.float32
BF16 = jnp.bfloat16

LOW = 12.0
STEPS = 32766.0 / (LOW + 15.25)


def polynomial(values, powers):
    spots = np.cos(np.pi * (np.arange(400) + 0.5) / 800) * 0.5
    table = np.stack([spots**power for power in powers], axis=1)
    return [float(c) for c in np.linalg.lstsq(table, values(np.pi * spots), rcond=None)[0]]


SIN_TERMS = polynomial(np.sin, (1, 3, 5, 7))
COS_TERMS = polynomial(np.cos, (0, 2, 4, 6))


def halves(table):
    high = table.astype(ml_dtypes.bfloat16)
    low = (table - high.astype(np.float64)).astype(ml_dtypes.bfloat16)
    return high, low


def angles(left, right, total):
    turns = np.outer(np.arange(left), np.arange(right)) % total
    return 2.0 * math.pi * turns / total


def stacked(table):
    high, low = halves(table)
    return np.block([[high, high], [low, np.zeros_like(low)]])


def tables():
    first = angles(64, 64, 64)
    turn = np.block([[np.cos(first), np.sin(first)], [-np.sin(first), np.cos(first)]])
    twist = angles(64, 128, GRID)
    second = angles(128, 128, 128)
    long_turn = np.block([[np.cos(second), -np.sin(second)], [np.sin(second), np.cos(second)]])
    return (
        stacked(turn),
        np.stack([np.cos(twist), np.sin(twist)]).astype(np.float32),
        np.stack(halves(long_turn)),
        stacked(turn / GRID),
    )


def split(value):
    high = value.astype(BF16)
    return high, (value - high.astype(F32)).astype(BF16)


def dot(left, right):
    return jnp.dot(left, right, preferred_element_type=F32)


def dot_short(table, value):
    high, low = split(value)
    both = dot(table, jnp.concatenate([high, low], axis=0))
    return both[:128] + both[128:]


def dot_long(value, tables):
    high, low = split(value)
    return dot(high, tables[0]) + dot(high, tables[1]) + dot(low, tables[0])


def gather_kernel(
    basis_hbm,
    coeff_hbm,
    reflect_hbm,
    row_hbm,
    column_hbm,
    live_hbm,
    near_ref,
    basis_ref,
    canvas_ref,
    coeff_ref,
    reflect_ref,
    row_ref,
    column_ref,
    live_ref,
    own,
    basis_sem,
    in_sem,
    send_sem,
    recv_sem,
):
    sector = lax.axis_index("sector")
    slab = lax.axis_index("slab")
    barrier = pltpu.get_barrier_semaphore()
    used = pl.ds(FIRST * TILE, (LAST - FIRST) * TILE)
    basis_copy = pltpu.make_async_copy(basis_hbm.at[:, used], basis_ref, basis_sem)
    sources = (coeff_hbm, reflect_hbm, row_hbm, column_hbm, live_hbm)
    held = (coeff_ref, reflect_ref, row_ref, column_ref, live_ref)
    loads = [
        pltpu.make_async_copy(one, two, in_sem.at[number])
        for number, (one, two) in enumerate(zip(sources, held))
    ]
    for load in loads:
        load.start()
    basis_copy.start()
    others = [(flip, hop) for hop in range(3) for flip in range(2)][1:]
    for flip, hop in others:
        for step in {hop, -hop}:
            pl.semaphore_signal(
                barrier,
                inc=1,
                device_id=(lax.rem(sector + flip, 2), lax.rem(slab + step + SLABS, SLABS)),
                device_id_type=MESH,
            )
    for load in loads:
        load.wait()
    own[:SLOTS, :MODES] = coeff_ref[...].astype(F32)
    for number, ref in enumerate((reflect_ref, row_ref, column_ref, live_ref)):
        own[SLOTS + number : SLOTS + number + 1, :SLOTS] = ref[...].astype(F32)
    near_ref[0, sector] = own[...]
    pl.semaphore_wait(barrier, 9)
    copies = []
    for number, (flip, hop) in enumerate(others):
        copy = pltpu.make_async_remote_copy(
            src_ref=own,
            dst_ref=near_ref.at[hop, sector],
            send_sem=send_sem.at[number],
            recv_sem=recv_sem.at[number],
            device_id=(lax.rem(sector + flip, 2), lax.rem(slab + hop, SLABS)),
            device_id_type=MESH,
        )
        copy.start()
        copies.append(copy)
    canvas_ref[...] = jnp.zeros_like(canvas_ref)
    for copy in copies:
        copy.wait()
    basis_copy.wait()


def gather_near(mode_basis, mode_coeff, *lists):
    vmem = pl.BlockSpec(memory_space=pltpu.VMEM)
    values = [mode_basis, mode_coeff] + [one.reshape(1, SLOTS) for one in lists]
    return pl.pallas_call(
        gather_kernel,
        out_shape=[
            jax.ShapeDtypeStruct((3, 2, SLOTS + 8, 128), F32),
            jax.ShapeDtypeStruct((MODES, (LAST - FIRST) * TILE), BF16),
            jax.ShapeDtypeStruct((2 * BLOCKS, WIDE, 128), F32),
        ],
        in_specs=[pl.BlockSpec(memory_space=pltpu.HBM)] * 6,
        out_specs=[vmem, vmem, vmem],
        scratch_shapes=[
            pltpu.VMEM((SLOTS, MODES), BF16),
            pltpu.VMEM((1, SLOTS), BF16),
            pltpu.VMEM((1, SLOTS), jnp.int32),
            pltpu.VMEM((1, SLOTS), jnp.int32),
            pltpu.VMEM((1, SLOTS), jnp.int32),
            pltpu.VMEM((SLOTS + 8, 128), F32),
            pltpu.SemaphoreType.DMA,
            pltpu.SemaphoreType.DMA((5,)),
            pltpu.SemaphoreType.DMA((5,)),
            pltpu.SemaphoreType.DMA((5,)),
        ],
        compiler_params=pltpu.CompilerParams(
            collective_id=0, has_side_effects=True, vmem_limit_bytes=20 << 20
        ),
        name="gather_near",
    )(*(pltpu.with_memory_space_constraint(value, pltpu.HBM) for value in values))


def circle(phase):
    turns = phase * (0.5 / math.pi)
    part = turns - jnp.round(turns)
    square = part * part
    sine = SIN_TERMS[-1]
    for term in SIN_TERMS[-2::-1]:
        sine = sine * square + term
    sine = sine * part
    cosine = COS_TERMS[-1]
    for term in COS_TERMS[-2::-1]:
        cosine = cosine * square + term
    double = sine + sine
    return 1.0 - double * sine, double * cosine


TOGETHER = 28
STEPS_EACH = (LAST - FIRST) // 2 // TOGETHER
LISTED = NEAR // STEPS_EACH
TASKS = 4


def render_kernel(
    near, basis, clear, canvas, left, right, marks, slots, table, tasks, slots_sem, table_sem
):
    sector = lax.axis_index("sector")
    slab = lax.axis_index("slab")
    base_row = 2 * LINES * slab + LINES * sector
    slots_copy = pltpu.make_async_copy(near.at[:, :, pl.ds(SLOTS, 8)], slots, slots_sem)
    slots_copy.start()
    for hop in range(3):
        for side in range(2):
            tile_row, column, live = (
                near[hop, side, SLOTS + number : SLOTS + number + 1, :].astype(jnp.int32)
                for number in (1, 2, 3)
            )
            top = base_row - tile_row
            at = 2 * hop + side
            marks[at, 0:1, :] = top
            marks[at, 1:2, :] = column >> 7
            marks[at, 2:3, :] = column & 127
            for part in range(2):
                start = top + part * HALF
                reaches = (start >= 17 - (HALF - 1)) & (start <= 238) & (live > 0)
                marks[at, 3 + part : 4 + part, :] = reaches.astype(jnp.int32)
    table_copy = pltpu.make_async_copy(marks, table, table_sem)
    table_copy.start()
    coeff = [
        jnp.concatenate([near[hop, side, :SLOTS, :MODES] for side in range(2)], axis=0).astype(BF16)
        for hop in range(3)
    ]

    def form(part, step):
        mix = jnp.concatenate([coeff[2 * part], coeff[1]], axis=0)
        row = (part * STEPS_EACH + step) * TOGETHER
        columns = pl.ds(pl.multiple_of(row * TILE, TOGETHER * TILE), TOGETHER * TILE)
        phases = dot(mix, basis[:, columns])
        for extra in range(TOGETHER):
            place = pl.ds(pl.multiple_of((row + extra + FIRST + PAD) * WIDE, 8), 64)
            at = extra * TILE
            left[place, :] = phases[:, at : at + 128]
            right[place, :] = phases[:, at + 128 : at + 256]

    @pl.loop(0, STEPS_EACH)
    def _(step):
        form(0, step)

    table_copy.wait()
    slots_copy.wait()

    def form_and_list(step, count):
        form(1, step)
        for extra in range(LISTED):
            slot = step * LISTED + extra
            for part in range(2):
                tasks[count] = 2 * slot + part
                count = count + table[slot >> 4, 3 + part, slot & 15]
        return count

    count = lax.fori_loop(0, STEPS_EACH, form_and_list, 0)
    lane = lax.broadcasted_iota(jnp.int32, (1, 128), 1)
    down = lax.broadcasted_iota(jnp.int32, (HALF, 1), 0)
    reach = 7 * (TILE - 2)

    def tile_part(number):
        task = tasks[jnp.minimum(number, count - 1)]
        slot = task >> 1
        part = task & 1
        group = slot >> 4
        at = slot & 15
        weight = jnp.where(number < count, slots[slot >> 5, group & 1, 0, at], 0.0)
        top = table[group, 0, at] + part * HALF
        block = table[group, 1, at]
        shift = table[group, 2, at]
        start = (top + PAD) * WIDE + (slot & 63)
        vertical = jnp.abs(2 * (top + down) - (TILE - 1))
        vertical = jnp.where(8 * vertical <= reach, 4 * vertical, 4 * reach)
        vertical = jnp.broadcast_to(vertical, (HALF, 128))
        place = (lane - shift) & 127
        room_left = reach - 7 * ((TILE - 1) - 2 * place)
        room_right = reach - 7 * (2 * place + 1)
        both = []
        for ref, room in ((left, room_left), (right, room_right)):
            wave = pltpu.roll(ref[pl.ds(start, HALF, stride=WIDE), :], shift, 1)
            inside = vertical <= room
            amplitude = jnp.where(inside, weight, 0.0)
            cosine, sine = circle(jnp.where(inside, wave, 0.0))
            both.append((cosine * amplitude, sine * amplitude))
        rows = pl.ds(pl.multiple_of(part * HALF, HALF), HALF)
        return block, rows, jnp.broadcast_to(lane >= shift, (HALF, 128)), both

    def deposit(block, rows, kept, both):
        for comp in range(2):
            one, two = both[0][comp], both[1][comp]
            at = comp * BLOCKS + block
            past = jnp.minimum(at + 2, 2 * BLOCKS - 1)
            canvas[at, rows, :] += jnp.where(kept, one, 0.0)
            canvas[at + 1, rows, :] += jnp.where(kept, two, one)
            canvas[past, rows, :] += jnp.where(kept, 0.0, two)

    @pl.loop(0, (count + TASKS - 1) // TASKS)
    def _(step):
        before = None
        for extra in range(TASKS):
            piece = tile_part(TASKS * step + extra)
            if before is not None:
                deposit(*before)
            before = piece
        deposit(*before)


def render(near, basis, clear):
    vmem = pl.BlockSpec(memory_space=pltpu.VMEM)
    return pl.pallas_call(
        render_kernel,
        out_shape=jax.ShapeDtypeStruct((2 * BLOCKS, WIDE, 128), F32),
        in_specs=[vmem, vmem, vmem],
        out_specs=vmem,
        input_output_aliases={2: 0},
        scratch_shapes=[
            pltpu.VMEM(((TILE + 2 * PAD) * WIDE, 128), F32),
            pltpu.VMEM(((TILE + 2 * PAD) * WIDE, 128), F32),
            pltpu.VMEM((6, 8, 128), jnp.int32),
            pltpu.SMEM((3, 2, 8, 128), F32),
            pltpu.SMEM((6, 8, 128), jnp.int32),
            pltpu.SMEM((2 * NEAR + 8,), jnp.int32),
            pltpu.SemaphoreType.DMA,
            pltpu.SemaphoreType.DMA,
        ],
        compiler_params=pltpu.CompilerParams(vmem_limit_bytes=40 << 20),
        name="render_rows",
    )(near, basis, clear)


def encode(value):
    size = jnp.log(jnp.abs(value)) * (STEPS / math.log(2.0)) + (LOW * STEPS + 0.5)
    code = jnp.maximum(size, 0.0).astype(jnp.int32)
    return jnp.where(value < 0.0, -code, code)


def decode(code):
    size = jnp.abs(code).astype(F32) * (math.log(2.0) / STEPS) - LOW * math.log(2.0)
    value = jnp.exp(size)
    return jnp.where(code == 0, 0.0, jnp.where(code < 0, -value, value))


def exchange_kernel(
    field,
    turn,
    twist,
    long_turn,
    mid_ref,
    wide,
    box,
    handed,
    early,
    inbox,
    plain,
    send_sem,
    recv_sem,
    swap_send_sem,
    swap_recv_sem,
):
    sector = lax.axis_index("sector")
    slab = lax.axis_index("slab")
    other_sector = 1 - sector
    barrier = pltpu.get_barrier_semaphore()

    def greet(target):
        pl.semaphore_signal(barrier, inc=1, device_id=target, device_id_type=MESH)

    greet((other_sector, slab))

    @pl.loop(1, SLABS, unroll=9)
    def _(step):
        greet((sector, (slab + step) & (SLABS - 1)))

    def swap(chunk):
        return pltpu.make_async_remote_copy(
            src_ref=early.at[:, other_sector] if chunk == 0 else handed.at[chunk - 1],
            dst_ref=(inbox if chunk == 0 else box).at[chunk, :, sector],
            send_sem=swap_send_sem.at[chunk],
            recv_sem=swap_recv_sem.at[chunk],
            device_id=(other_sector, slab),
            device_id_type=MESH,
        )

    lines = field.reshape(2 * BLOCKS * WIDE, 128)
    codes = wide.reshape(DEVICES * SHORT, 128)
    values = plain.reshape(DEVICES * SHORT, 128)
    for chunk in range(CHUNKS):

        @pl.loop(0, CHUNK // 4)
        def _(step):
            parts = []
            for pair in range(2):
                line = chunk * CHUNK + 4 * step + 2 * pair
                both = [lines[pl.ds(line + e, 2 * BLOCKS, stride=WIDE), :] for e in range(2)]
                mid = dot_short(turn[...], jnp.concatenate(both, axis=1))
                for e in range(2):
                    real = mid[:64, 128 * e : 128 * e + 128]
                    imag = mid[64:, 128 * e : 128 * e + 128]
                    turned_real = real * twist[0] + imag * twist[1]
                    turned_imag = imag * twist[0] - real * twist[1]
                    parts.append(jnp.concatenate([turned_real, turned_imag], axis=1))
            done = encode(dot_long(jnp.concatenate(parts, axis=0), long_turn))
            for e in range(4):
                some = done[64 * e : 64 * e + 64]
                some = jnp.concatenate([some[:, :128], some[:, 128:]], axis=0).T
                codes[pl.ds(4 * step + e, DEVICES, stride=SHORT), :] = some

        @pl.loop(0, SLABS // 16)
        def _(step):
            some = pl.ds(step * 16, 16)
            for side, to in ((sector, sector), (other_sector, other_sector)):
                packed = wide[pl.ds(to * SLABS + step * 16, 16), :CHUNK].astype(jnp.int16)
                if chunk > 0 and side is other_sector:
                    handed[chunk - 1, some] = packed
                else:
                    box[chunk, some, side] = packed

        if chunk == 0:
            pl.semaphore_wait(barrier, SLABS)
        else:
            swap(chunk).start()
            swap(chunk).wait()
        land = early if chunk == 0 else inbox.at[chunk]

        @pl.loop(1, SLABS, unroll=3)
        def _(step):
            target = (slab + step) & (SLABS - 1)
            pltpu.make_async_remote_copy(
                src_ref=box.at[chunk, target],
                dst_ref=land.at[slab],
                send_sem=send_sem.at[chunk],
                recv_sem=recv_sem.at[chunk],
                device_id=(sector, target),
                device_id_type=MESH,
            ).start()

        land[slab] = box[chunk, slab]

    for chunk in range(CHUNKS):
        most = (early if chunk == 0 else inbox.at[chunk]).at[pl.ds(0, SLABS - 1)]
        pltpu.make_async_copy(most, most, recv_sem.at[chunk]).wait()
        if chunk == 0:
            swap(0).start()
            inbox[0, :, sector] = early[:, sector]
            swap(0).wait()

        @pl.loop(0, DEVICES // 16, unroll=4)
        def _(step):
            codes_in = inbox[chunk, pl.ds(step * 8, 8)].astype(jnp.int32)
            plain[pl.ds(step * 16, 16), :CHUNK] = decode(codes_in).reshape(16, CHUNK, 128)

        @pl.loop(0, CHUNK // 8)
        def _(step):
            parts = []
            for e in range(8):
                turned = values[pl.ds(8 * step + e, DEVICES, stride=SHORT), :].T
                parts.append(jnp.concatenate([turned[:64], turned[64:]], axis=1))
            mid = dot_long(jnp.concatenate(parts, axis=0), long_turn)
            for e in range(8):
                line = chunk * CHUNK + 8 * step + e
                cos = twist[0, pl.ds(line, 1), :]
                sin = twist[1, pl.ds(line, 1), :]
                real = mid[64 * e : 64 * e + 64, :128]
                imag = mid[64 * e : 64 * e + 64, 128:]
                mid_ref[0, line, :LINES] = real * cos + imag * sin
                mid_ref[1, line, :LINES] = imag * cos - real * sin

    for chunk in range(CHUNKS):
        most = box.at[chunk, pl.ds(0, SLABS - 1)]
        pltpu.make_async_copy(most, most, send_sem.at[chunk]).wait()


def exchange(field, *consts):
    vmem = pl.BlockSpec(memory_space=pltpu.VMEM)
    return pl.pallas_call(
        exchange_kernel,
        out_shape=jax.ShapeDtypeStruct((2, LINES, WIDE, 128), F32),
        in_specs=[vmem] * 4,
        out_specs=vmem,
        scratch_shapes=[
            pltpu.VMEM((DEVICES, SHORT, 128), jnp.int32),
            pltpu.VMEM((CHUNKS, SLABS, 2, CHUNK, 128), jnp.int16),
            pltpu.VMEM((CHUNKS - 1, SLABS, CHUNK, 128), jnp.int16),
            pltpu.VMEM((SLABS, 2, CHUNK, 128), jnp.int16),
            pltpu.VMEM((CHUNKS, SLABS, 2, CHUNK, 128), jnp.int16),
            pltpu.VMEM((DEVICES, SHORT, 128), F32),
            pltpu.SemaphoreType.DMA((CHUNKS,)),
            pltpu.SemaphoreType.DMA((CHUNKS,)),
            pltpu.SemaphoreType.DMA((CHUNKS,)),
            pltpu.SemaphoreType.DMA((CHUNKS,)),
        ],
        compiler_params=pltpu.CompilerParams(
            collective_id=1, has_side_effects=True, vmem_limit_bytes=32 << 20
        ),
        name="exchange",
    )(field, *consts)


def finish_kernel(mid_ref, turn, out_hbm, turned, ready, out_sem):
    lines = mid_ref.reshape(2 * LINES * WIDE, 128)

    def leave(group):
        rows = pl.ds(group * 8, 8)
        return pltpu.make_async_copy(ready.at[:, rows], out_hbm.at[:, rows], out_sem.at[group])

    for group in range(LINES // 8):
        for pair in range(4):
            line = group * 8 + 2 * pair
            both = [lines[pl.ds(line + e, 2 * LINES, stride=WIDE), :] for e in range(2)]
            done = dot_short(turn[...], jnp.concatenate(both, axis=1))
            for e in range(2):
                turned[group % 2, pl.ds(2 * pair + e, 2 * LINES, stride=8), :] = done[
                    :, 128 * e : 128 * e + 128
                ]
        for comp in range(2):
            for block in range(LINES):
                at = (comp * LINES + block) * 8
                ready[comp, 8 * group : 8 * group + 8, 128 * block : 128 * block + 128] = turned[
                    group % 2, at : at + 8, :
                ]
        leave(group).start()
    for group in range(LINES // 8):
        leave(group).wait()


def finish(mid, turn):
    vmem = pl.BlockSpec(memory_space=pltpu.VMEM)
    return pl.pallas_call(
        finish_kernel,
        out_shape=jax.ShapeDtypeStruct((2, LINES, GRID), F32),
        in_specs=[vmem, vmem],
        out_specs=pl.BlockSpec(memory_space=pl.ANY),
        scratch_shapes=[
            pltpu.VMEM((2, 2 * LINES * 8, 128), F32),
            pltpu.VMEM((2, LINES, GRID), F32),
            pltpu.SemaphoreType.DMA((LINES // 8,)),
        ],
        compiler_params=pltpu.CompilerParams(vmem_limit_bytes=24 << 20),
        name="finish",
    )(mid, turn)


def body(mode_basis, mode_coeff, reflect, tile_row, tile_col, slot_live):
    turn, twist, long_turn, last_turn = (jnp.asarray(table) for table in tables())
    near, basis, clear = gather_near(
        mode_basis, mode_coeff, reflect, tile_row, tile_col, slot_live
    )
    field = render(near, basis, clear)
    mid = exchange(field, turn, twist, long_turn)
    return finish(mid, last_turn)


def solution(mesh):
    placed = (
        P(),
        P(("sector", "slab"), None),
        P(("sector", "slab")),
        P(("sector", "slab")),
        P(("sector", "slab")),
        P(("sector", "slab")),
    )
    return jax.shard_map(
        body,
        mesh=mesh,
        in_specs=placed,
        out_specs=P(None, ("sector", "slab"), None),
        check_vma=False,
    )
```

```python
import functools
import math

import jax
import jax.numpy as jnp
import ml_dtypes
import numpy as np
from jax import lax
from jax.experimental import pallas as pl
from jax.experimental.pallas import tpu as pltpu
from jax.sharding import PartitionSpec as P

GRID = 8192
TILE = 256
SLOTS = 16
MODES = 64
SLABS = 64
DEVICES = 128
LINES = GRID // DEVICES
BLOCKS = GRID // 128
NEAR = 6 * SLOTS
CHUNK = 16
CHUNKS = LINES // CHUNK
PAD = 16
HALF = 32
FIRST, LAST = 16, 240
WIDE = LINES + 8
SHORT = CHUNK + 8
MESH = pl.DeviceIdType.MESH
F32 = jnp.float32
BF16 = jnp.bfloat16

LOW = 12.0
STEPS = 32766.0 / (LOW + 15.25)


def polynomial(values, powers):
    spots = np.cos(np.pi * (np.arange(400) + 0.5) / 800) * 0.5
    table = np.stack([spots**power for power in powers], axis=1)
    return [float(c) for c in np.linalg.lstsq(table, values(np.pi * spots), rcond=None)[0]]


SIN_TERMS = polynomial(np.sin, (1, 3, 5, 7))
COS_TERMS = polynomial(np.cos, (0, 2, 4, 6))


def halves(table):
    high = table.astype(ml_dtypes.bfloat16)
    low = (table - high.astype(np.float64)).astype(ml_dtypes.bfloat16)
    return high, low


def angles(left, right, total):
    turns = np.outer(np.arange(left), np.arange(right)) % total
    return 2.0 * math.pi * turns / total


def stacked(table):
    high, low = halves(table)
    return np.block([[high, high], [low, np.zeros_like(low)]])


def tables():
    first = angles(64, 64, 64)
    turn = np.block([[np.cos(first), np.sin(first)], [-np.sin(first), np.cos(first)]])
    twist = angles(64, 128, GRID)
    second = angles(128, 128, 128)
    long_turn = np.block([[np.cos(second), -np.sin(second)], [np.sin(second), np.cos(second)]])
    return (
        stacked(turn),
        np.stack([np.cos(twist), np.sin(twist)]).astype(np.float32),
        np.stack(halves(long_turn)),
        stacked(turn / GRID),
    )


def split(value):
    high = value.astype(BF16)
    return high, (value - high.astype(F32)).astype(BF16)


def dot(left, right):
    return jnp.dot(left, right, preferred_element_type=F32)


def dot_short(table, value):
    high, low = split(value)
    both = dot(table, jnp.concatenate([high, low], axis=0))
    return both[:128] + both[128:]


def dot_long(value, tables):
    high, low = split(value)
    return dot(high, tables[0]) + dot(high, tables[1]) + dot(low, tables[0])


def gather_kernel(
    basis_hbm,
    coeff_hbm,
    reflect_hbm,
    row_hbm,
    column_hbm,
    live_hbm,
    near_ref,
    basis_ref,
    canvas_ref,
    coeff_ref,
    reflect_ref,
    row_ref,
    column_ref,
    live_ref,
    own,
    basis_sem,
    in_sem,
    send_sem,
    recv_sem,
):
    sector = lax.axis_index("sector")
    slab = lax.axis_index("slab")
    barrier = pltpu.get_barrier_semaphore()
    used = pl.ds(FIRST * TILE, (LAST - FIRST) * TILE)
    basis_copy = pltpu.make_async_copy(basis_hbm.at[:, used], basis_ref, basis_sem)
    sources = (coeff_hbm, reflect_hbm, row_hbm, column_hbm, live_hbm)
    held = (coeff_ref, reflect_ref, row_ref, column_ref, live_ref)
    loads = [
        pltpu.make_async_copy(one, two, in_sem.at[number])
        for number, (one, two) in enumerate(zip(sources, held))
    ]
    for load in loads:
        load.start()
    basis_copy.start()
    others = [(flip, hop) for hop in range(3) for flip in range(2)][1:]
    for flip, hop in others:
        for step in {hop, -hop}:
            pl.semaphore_signal(
                barrier,
                inc=1,
                device_id=(lax.rem(sector + flip, 2), lax.rem(slab + step + SLABS, SLABS)),
                device_id_type=MESH,
            )
    for load in loads:
        load.wait()
    own[:SLOTS, :MODES] = coeff_ref[...].astype(F32)
    for number, ref in enumerate((reflect_ref, row_ref, column_ref, live_ref)):
        own[SLOTS + number : SLOTS + number + 1, :SLOTS] = ref[...].astype(F32)
    near_ref[0, sector] = own[...]
    pl.semaphore_wait(barrier, 9)
    copies = []
    for number, (flip, hop) in enumerate(others):
        copy = pltpu.make_async_remote_copy(
            src_ref=own,
            dst_ref=near_ref.at[hop, sector],
            send_sem=send_sem.at[number],
            recv_sem=recv_sem.at[number],
            device_id=(lax.rem(sector + flip, 2), lax.rem(slab + hop, SLABS)),
            device_id_type=MESH,
        )
        copy.start()
        copies.append(copy)
    canvas_ref[...] = jnp.zeros_like(canvas_ref)
    for copy in copies:
        copy.wait()
    basis_copy.wait()


def gather_near(mode_basis, mode_coeff, *lists):
    vmem = pl.BlockSpec(memory_space=pltpu.VMEM)
    values = [mode_basis, mode_coeff] + [one.reshape(1, SLOTS) for one in lists]
    return pl.pallas_call(
        gather_kernel,
        out_shape=[
            jax.ShapeDtypeStruct((3, 2, SLOTS + 8, 128), F32),
            jax.ShapeDtypeStruct((MODES, (LAST - FIRST) * TILE), BF16),
            jax.ShapeDtypeStruct((2 * BLOCKS, WIDE, 128), F32),
        ],
        in_specs=[pl.BlockSpec(memory_space=pltpu.HBM)] * 6,
        out_specs=[vmem, vmem, vmem],
        scratch_shapes=[
            pltpu.VMEM((SLOTS, MODES), BF16),
            pltpu.VMEM((1, SLOTS), BF16),
            pltpu.VMEM((1, SLOTS), jnp.int32),
            pltpu.VMEM((1, SLOTS), jnp.int32),
            pltpu.VMEM((1, SLOTS), jnp.int32),
            pltpu.VMEM((SLOTS + 8, 128), F32),
            pltpu.SemaphoreType.DMA,
            pltpu.SemaphoreType.DMA((5,)),
            pltpu.SemaphoreType.DMA((5,)),
            pltpu.SemaphoreType.DMA((5,)),
        ],
        compiler_params=pltpu.CompilerParams(
            collective_id=0, has_side_effects=True, vmem_limit_bytes=20 << 20
        ),
        name="gather_near",
    )(*(pltpu.with_memory_space_constraint(value, pltpu.HBM) for value in values))


def circle(phase):
    turns = phase * (0.5 / math.pi)
    part = turns - jnp.round(turns)
    square = part * part
    sine = SIN_TERMS[-1]
    for term in SIN_TERMS[-2::-1]:
        sine = sine * square + term
    sine = sine * part
    cosine = COS_TERMS[-1]
    for term in COS_TERMS[-2::-1]:
        cosine = cosine * square + term
    double = sine + sine
    return 1.0 - double * sine, double * cosine


TOGETHER = 56
STEPS_EACH = (LAST - FIRST) // 2 // TOGETHER
LISTED = NEAR // STEPS_EACH
TASKS = 8


def render_kernel(
    near, basis, clear, canvas, left, right, marks, slots, table, tasks, slots_sem, table_sem
):
    sector = lax.axis_index("sector")
    slab = lax.axis_index("slab")
    base_row = 2 * LINES * slab + LINES * sector
    slots_copy = pltpu.make_async_copy(near.at[:, :, pl.ds(SLOTS, 8)], slots, slots_sem)
    slots_copy.start()
    for hop in range(3):
        for side in range(2):
            tile_row, column, live = (
                near[hop, side, SLOTS + number : SLOTS + number + 1, :].astype(jnp.int32)
                for number in (1, 2, 3)
            )
            top = base_row - tile_row
            at = 2 * hop + side
            marks[at, 0:1, :] = top
            marks[at, 1:2, :] = column >> 7
            marks[at, 2:3, :] = column & 127
            for part in range(2):
                start = top + part * HALF
                reaches = (start >= 17 - (HALF - 1)) & (start <= 238) & (live > 0)
                marks[at, 3 + part : 4 + part, :] = reaches.astype(jnp.int32)
    table_copy = pltpu.make_async_copy(marks, table, table_sem)
    table_copy.start()
    coeff = [
        jnp.concatenate([near[hop, side, :SLOTS, :MODES] for side in range(2)], axis=0).astype(BF16)
        for hop in range(3)
    ]

    def form(part, step):
        mix = jnp.concatenate([coeff[2 * part], coeff[1]], axis=0)
        row = (part * STEPS_EACH + step) * TOGETHER
        columns = pl.ds(pl.multiple_of(row * TILE, TOGETHER * TILE), TOGETHER * TILE)
        phases = dot(mix, basis[:, columns])
        for extra in range(TOGETHER):
            place = pl.ds(pl.multiple_of((row + extra + FIRST + PAD) * WIDE, 8), 64)
            at = extra * TILE
            left[place, :] = phases[:, at : at + 128]
            right[place, :] = phases[:, at + 128 : at + 256]

    @pl.loop(0, STEPS_EACH)
    def _(step):
        form(0, step)

    table_copy.wait()
    slots_copy.wait()

    def form_and_list(step, count):
        form(1, step)
        for extra in range(LISTED):
            slot = step * LISTED + extra
            for part in range(2):
                tasks[count] = 2 * slot + part
                count = count + table[slot >> 4, 3 + part, slot & 15]
        return count

    count = lax.fori_loop(0, STEPS_EACH, form_and_list, 0)
    lane = lax.broadcasted_iota(jnp.int32, (1, 128), 1)
    down = lax.broadcasted_iota(jnp.int32, (HALF, 1), 0)
    reach = 7 * (TILE - 2)

    def tile_part(number):
        task = tasks[jnp.minimum(number, count - 1)]
        slot = task >> 1
        part = task & 1
        group = slot >> 4
        at = slot & 15
        weight = jnp.where(number < count, slots[slot >> 5, group & 1, 0, at], 0.0)
        top = table[group, 0, at] + part * HALF
        block = table[group, 1, at]
        shift = table[group, 2, at]
        start = (top + PAD) * WIDE + (slot & 63)
        vertical = jnp.abs(2 * (top + down) - (TILE - 1))
        vertical = jnp.where(8 * vertical <= reach, 4 * vertical, 4 * reach)
        vertical = jnp.broadcast_to(vertical, (HALF, 128))
        place = (lane - shift) & 127
        room_left = reach - 7 * ((TILE - 1) - 2 * place)
        room_right = reach - 7 * (2 * place + 1)
        both = []
        for ref, room in ((left, room_left), (right, room_right)):
            wave = pltpu.roll(ref[pl.ds(start, HALF, stride=WIDE), :], shift, 1)
            inside = vertical <= room
            amplitude = jnp.where(inside, weight, 0.0)
            cosine, sine = circle(jnp.where(inside, wave, 0.0))
            both.append((cosine * amplitude, sine * amplitude))
        rows = pl.ds(pl.multiple_of(part * HALF, HALF), HALF)
        return block, rows, jnp.broadcast_to(lane >= shift, (HALF, 128)), both

    def deposit(block, rows, kept, both):
        for comp in range(2):
            one, two = both[0][comp], both[1][comp]
            at = comp * BLOCKS + block
            past = jnp.minimum(at + 2, 2 * BLOCKS - 1)
            canvas[at, rows, :] += jnp.where(kept, one, 0.0)
            canvas[at + 1, rows, :] += jnp.where(kept, two, one)
            canvas[past, rows, :] += jnp.where(kept, 0.0, two)

    @pl.loop(0, (count + TASKS - 1) // TASKS)
    def _(step):
        before = None
        for extra in range(TASKS):
            piece = tile_part(TASKS * step + extra)
            if before is not None:
                deposit(*before)
            before = piece
        deposit(*before)


def render(near, basis, clear):
    vmem = pl.BlockSpec(memory_space=pltpu.VMEM)
    return pl.pallas_call(
        render_kernel,
        out_shape=jax.ShapeDtypeStruct((2 * BLOCKS, WIDE, 128), F32),
        in_specs=[vmem, vmem, vmem],
        out_specs=vmem,
        input_output_aliases={2: 0},
        scratch_shapes=[
            pltpu.VMEM(((TILE + 2 * PAD) * WIDE, 128), F32),
            pltpu.VMEM(((TILE + 2 * PAD) * WIDE, 128), F32),
            pltpu.VMEM((6, 8, 128), jnp.int32),
            pltpu.SMEM((3, 2, 8, 128), F32),
            pltpu.SMEM((6, 8, 128), jnp.int32),
            pltpu.SMEM((2 * NEAR + 8,), jnp.int32),
            pltpu.SemaphoreType.DMA,
            pltpu.SemaphoreType.DMA,
        ],
        compiler_params=pltpu.CompilerParams(vmem_limit_bytes=40 << 20),
        name="render_rows",
    )(near, basis, clear)


def encode(value):
    size = jnp.log(jnp.abs(value)) * (STEPS / math.log(2.0)) + (LOW * STEPS + 0.5)
    code = jnp.maximum(size, 0.0).astype(jnp.int32)
    return jnp.where(value < 0.0, -code, code)


def decode(code):
    size = jnp.abs(code).astype(F32) * (math.log(2.0) / STEPS) - LOW * math.log(2.0)
    value = jnp.exp(size)
    return jnp.where(code == 0, 0.0, jnp.where(code < 0, -value, value))


def exchange_kernel(
    field,
    turn,
    twist,
    long_turn,
    mid_ref,
    wide,
    box,
    handed,
    early,
    inbox,
    plain,
    send_sem,
    recv_sem,
    swap_send_sem,
    swap_recv_sem,
):
    sector = lax.axis_index("sector")
    slab = lax.axis_index("slab")
    other_sector = 1 - sector
    barrier = pltpu.get_barrier_semaphore()

    def greet(target):
        pl.semaphore_signal(barrier, inc=1, device_id=target, device_id_type=MESH)

    greet((other_sector, slab))

    @pl.loop(1, SLABS, unroll=21)
    def _(step):
        greet((sector, (slab + step) & (SLABS - 1)))

    def swap(chunk):
        return pltpu.make_async_remote_copy(
            src_ref=early.at[:, other_sector] if chunk == 0 else handed.at[chunk - 1],
            dst_ref=(inbox if chunk == 0 else box).at[chunk, :, sector],
            send_sem=swap_send_sem.at[chunk],
            recv_sem=swap_recv_sem.at[chunk],
            device_id=(other_sector, slab),
            device_id_type=MESH,
        )

    lines = field.reshape(2 * BLOCKS * WIDE, 128)
    codes = wide.reshape(DEVICES * SHORT, 128)
    values = plain.reshape(DEVICES * SHORT, 128)
    for chunk in range(CHUNKS):

        @pl.loop(0, CHUNK // 4)
        def _(step):
            parts = []
            for pair in range(2):
                line = chunk * CHUNK + 4 * step + 2 * pair
                both = [lines[pl.ds(line + e, 2 * BLOCKS, stride=WIDE), :] for e in range(2)]
                mid = dot_short(turn[...], jnp.concatenate(both, axis=1))
                for e in range(2):
                    real = mid[:64, 128 * e : 128 * e + 128]
                    imag = mid[64:, 128 * e : 128 * e + 128]
                    turned_real = real * twist[0] + imag * twist[1]
                    turned_imag = imag * twist[0] - real * twist[1]
                    parts.append(jnp.concatenate([turned_real, turned_imag], axis=1))
            done = encode(dot_long(jnp.concatenate(parts, axis=0), long_turn))
            for e in range(4):
                some = done[64 * e : 64 * e + 64]
                some = jnp.concatenate([some[:, :128], some[:, 128:]], axis=0).T
                codes[pl.ds(4 * step + e, DEVICES, stride=SHORT), :] = some

        @pl.loop(0, SLABS // 16)
        def _(step):
            some = pl.ds(step * 16, 16)
            for side, to in ((sector, sector), (other_sector, other_sector)):
                packed = wide[pl.ds(to * SLABS + step * 16, 16), :CHUNK].astype(jnp.int16)
                if chunk > 0 and side is other_sector:
                    handed[chunk - 1, some] = packed
                else:
                    box[chunk, some, side] = packed

        if chunk == 0:
            pl.semaphore_wait(barrier, SLABS)
        else:
            swap(chunk).start()
            swap(chunk).wait()
        land = early if chunk == 0 else inbox.at[chunk]

        @pl.loop(1, SLABS, unroll=3)
        def _(step):
            target = (slab + step) & (SLABS - 1)
            pltpu.make_async_remote_copy(
                src_ref=box.at[chunk, target],
                dst_ref=land.at[slab],
                send_sem=send_sem.at[chunk],
                recv_sem=recv_sem.at[chunk],
                device_id=(sector, target),
                device_id_type=MESH,
            ).start()

        land[slab] = box[chunk, slab]

    for chunk in range(CHUNKS):
        most = (early if chunk == 0 else inbox.at[chunk]).at[pl.ds(0, SLABS - 1)]
        pltpu.make_async_copy(most, most, recv_sem.at[chunk]).wait()
        if chunk == 0:
            swap(0).start()
            inbox[0, :, sector] = early[:, sector]
            swap(0).wait()

        @pl.loop(0, DEVICES // 16, unroll=4)
        def _(step):
            codes_in = inbox[chunk, pl.ds(step * 8, 8)].astype(jnp.int32)
            plain[pl.ds(step * 16, 16), :CHUNK] = decode(codes_in).reshape(16, CHUNK, 128)

        @pl.loop(0, CHUNK // 8)
        def _(step):
            parts = []
            for e in range(8):
                turned = values[pl.ds(8 * step + e, DEVICES, stride=SHORT), :].T
                parts.append(jnp.concatenate([turned[:64], turned[64:]], axis=1))
            mid = dot_long(jnp.concatenate(parts, axis=0), long_turn)
            for e in range(8):
                line = chunk * CHUNK + 8 * step + e
                cos = twist[0, pl.ds(line, 1), :]
                sin = twist[1, pl.ds(line, 1), :]
                real = mid[64 * e : 64 * e + 64, :128]
                imag = mid[64 * e : 64 * e + 64, 128:]
                mid_ref[0, line, :LINES] = real * cos + imag * sin
                mid_ref[1, line, :LINES] = imag * cos - real * sin

    for chunk in range(CHUNKS):
        most = box.at[chunk, pl.ds(0, SLABS - 1)]
        pltpu.make_async_copy(most, most, send_sem.at[chunk]).wait()


def exchange(field, *consts):
    vmem = pl.BlockSpec(memory_space=pltpu.VMEM)
    return pl.pallas_call(
        exchange_kernel,
        out_shape=jax.ShapeDtypeStruct((2, LINES, WIDE, 128), F32),
        in_specs=[vmem] * 4,
        out_specs=vmem,
        scratch_shapes=[
            pltpu.VMEM((DEVICES, SHORT, 128), jnp.int32),
            pltpu.VMEM((CHUNKS, SLABS, 2, CHUNK, 128), jnp.int16),
            pltpu.VMEM((CHUNKS - 1, SLABS, CHUNK, 128), jnp.int16),
            pltpu.VMEM((SLABS, 2, CHUNK, 128), jnp.int16),
            pltpu.VMEM((CHUNKS, SLABS, 2, CHUNK, 128), jnp.int16),
            pltpu.VMEM((DEVICES, SHORT, 128), F32),
            pltpu.SemaphoreType.DMA((CHUNKS,)),
            pltpu.SemaphoreType.DMA((CHUNKS,)),
            pltpu.SemaphoreType.DMA((CHUNKS,)),
            pltpu.SemaphoreType.DMA((CHUNKS,)),
        ],
        compiler_params=pltpu.CompilerParams(
            collective_id=1, has_side_effects=True, vmem_limit_bytes=32 << 20
        ),
        name="exchange",
    )(field, *consts)


def finish_kernel(mid_ref, turn, out_hbm, turned, ready, out_sem):
    lines = mid_ref.reshape(2 * LINES * WIDE, 128)

    def leave(group):
        rows = pl.ds(group * 8, 8)
        return pltpu.make_async_copy(ready.at[:, rows], out_hbm.at[:, rows], out_sem.at[group])

    for group in range(LINES // 8):
        for pair in range(4):
            line = group * 8 + 2 * pair
            both = [lines[pl.ds(line + e, 2 * LINES, stride=WIDE), :] for e in range(2)]
            done = dot_short(turn[...], jnp.concatenate(both, axis=1))
            for e in range(2):
                turned[group % 2, pl.ds(2 * pair + e, 2 * LINES, stride=8), :] = done[
                    :, 128 * e : 128 * e + 128
                ]
        for comp in range(2):
            for block in range(LINES):
                at = (comp * LINES + block) * 8
                ready[comp, 8 * group : 8 * group + 8, 128 * block : 128 * block + 128] = turned[
                    group % 2, at : at + 8, :
                ]
        leave(group).start()
    for group in range(LINES // 8):
        leave(group).wait()


def finish(mid, turn):
    vmem = pl.BlockSpec(memory_space=pltpu.VMEM)
    return pl.pallas_call(
        finish_kernel,
        out_shape=jax.ShapeDtypeStruct((2, LINES, GRID), F32),
        in_specs=[vmem, vmem],
        out_specs=pl.BlockSpec(memory_space=pl.ANY),
        scratch_shapes=[
            pltpu.VMEM((2, 2 * LINES * 8, 128), F32),
            pltpu.VMEM((2, LINES, GRID), F32),
            pltpu.SemaphoreType.DMA((LINES // 8,)),
        ],
        compiler_params=pltpu.CompilerParams(vmem_limit_bytes=24 << 20),
        name="finish",
    )(mid, turn)


def body(mode_basis, mode_coeff, reflect, tile_row, tile_col, slot_live):
    turn, twist, long_turn, last_turn = (jnp.asarray(table) for table in tables())
    near, basis, clear = gather_near(
        mode_basis, mode_coeff, reflect, tile_row, tile_col, slot_live
    )
    field = render(near, basis, clear)
    mid = exchange(field, turn, twist, long_turn)
    return finish(mid, last_turn)


def solution(mesh):
    placed = (
        P(),
        P(("sector", "slab"), None),
        P(("sector", "slab")),
        P(("sector", "slab")),
        P(("sector", "slab")),
        P(("sector", "slab")),
    )
    return jax.shard_map(
        body,
        mesh=mesh,
        in_specs=placed,
        out_specs=P(None, ("sector", "slab"), None),
        check_vma=False,
    )
```

```python
import functools
import math

import jax
import jax.numpy as jnp
import ml_dtypes
import numpy as np
from jax import lax
from jax.experimental import pallas as pl
from jax.experimental.pallas import tpu as pltpu
from jax.sharding import PartitionSpec as P

GRID = 8192
TILE = 256
SLOTS = 16
MODES = 64
SLABS = 64
DEVICES = 128
LINES = GRID // DEVICES
BLOCKS = GRID // 128
NEAR = 6 * SLOTS
CHUNK = 16
CHUNKS = LINES // CHUNK
PAD = 16
HALF = 32
FIRST, LAST = 16, 240
WIDE = LINES + 8
SHORT = CHUNK + 8
MESH = pl.DeviceIdType.MESH
F32 = jnp.float32
BF16 = jnp.bfloat16

LOW = 12.0
STEPS = 32766.0 / (LOW + 15.25)


def polynomial(values, powers):
    spots = np.cos(np.pi * (np.arange(400) + 0.5) / 800) * 0.5
    table = np.stack([spots**power for power in powers], axis=1)
    return [float(c) for c in np.linalg.lstsq(table, values(np.pi * spots), rcond=None)[0]]


SIN_TERMS = polynomial(np.sin, (1, 3, 5, 7))
COS_TERMS = polynomial(np.cos, (0, 2, 4, 6))


def halves(table):
    high = table.astype(ml_dtypes.bfloat16)
    low = (table - high.astype(np.float64)).astype(ml_dtypes.bfloat16)
    return high, low


def angles(left, right, total):
    turns = np.outer(np.arange(left), np.arange(right)) % total
    return 2.0 * math.pi * turns / total


def stacked(table):
    high, low = halves(table)
    return np.block([[high, high], [low, np.zeros_like(low)]])


def tables():
    first = angles(64, 64, 64)
    turn = np.block([[np.cos(first), np.sin(first)], [-np.sin(first), np.cos(first)]])
    twist = angles(64, 128, GRID)
    second = angles(128, 128, 128)
    long_turn = np.block([[np.cos(second), -np.sin(second)], [np.sin(second), np.cos(second)]])
    return (
        stacked(turn),
        np.stack([np.cos(twist), np.sin(twist)]).astype(np.float32),
        np.stack(halves(long_turn)),
        stacked(turn / GRID),
    )


def split(value):
    high = value.astype(BF16)
    return high, (value - high.astype(F32)).astype(BF16)


def dot(left, right):
    return jnp.dot(left, right, preferred_element_type=F32)


def dot_short(table, value):
    high, low = split(value)
    both = dot(table, jnp.concatenate([high, low], axis=0))
    return both[:128] + both[128:]


def dot_long(value, tables):
    high, low = split(value)
    return dot(high, tables[0]) + dot(high, tables[1]) + dot(low, tables[0])


def gather_kernel(
    basis_hbm,
    coeff_hbm,
    reflect_hbm,
    row_hbm,
    column_hbm,
    live_hbm,
    near_ref,
    basis_ref,
    canvas_ref,
    coeff_ref,
    reflect_ref,
    row_ref,
    column_ref,
    live_ref,
    own,
    basis_sem,
    in_sem,
    send_sem,
    recv_sem,
):
    sector = lax.axis_index("sector")
    slab = lax.axis_index("slab")
    barrier = pltpu.get_barrier_semaphore()
    used = pl.ds(FIRST * TILE, (LAST - FIRST) * TILE)
    basis_copy = pltpu.make_async_copy(basis_hbm.at[:, used], basis_ref, basis_sem)
    sources = (coeff_hbm, reflect_hbm, row_hbm, column_hbm, live_hbm)
    held = (coeff_ref, reflect_ref, row_ref, column_ref, live_ref)
    loads = [
        pltpu.make_async_copy(one, two, in_sem.at[number])
        for number, (one, two) in enumerate(zip(sources, held))
    ]
    for load in loads:
        load.start()
    basis_copy.start()
    others = [(flip, hop) for hop in range(3) for flip in range(2)][1:]
    for flip, hop in others:
        for step in {hop, -hop}:
            pl.semaphore_signal(
                barrier,
                inc=1,
                device_id=(lax.rem(sector + flip, 2), lax.rem(slab + step + SLABS, SLABS)),
                device_id_type=MESH,
            )
    for load in loads:
        load.wait()
    own[:SLOTS, :MODES] = coeff_ref[...].astype(F32)
    for number, ref in enumerate((reflect_ref, row_ref, column_ref, live_ref)):
        own[SLOTS + number : SLOTS + number + 1, :SLOTS] = ref[...].astype(F32)
    near_ref[0, sector] = own[...]
    pl.semaphore_wait(barrier, 9)
    copies = []
    for number, (flip, hop) in enumerate(others):
        copy = pltpu.make_async_remote_copy(
            src_ref=own,
            dst_ref=near_ref.at[hop, sector],
            send_sem=send_sem.at[number],
            recv_sem=recv_sem.at[number],
            device_id=(lax.rem(sector + flip, 2), lax.rem(slab + hop, SLABS)),
            device_id_type=MESH,
        )
        copy.start()
        copies.append(copy)
    canvas_ref[...] = jnp.zeros_like(canvas_ref)
    for copy in copies:
        copy.wait()
    basis_copy.wait()


def gather_near(mode_basis, mode_coeff, *lists):
    vmem = pl.BlockSpec(memory_space=pltpu.VMEM)
    values = [mode_basis, mode_coeff] + [one.reshape(1, SLOTS) for one in lists]
    return pl.pallas_call(
        gather_kernel,
        out_shape=[
            jax.ShapeDtypeStruct((3, 2, SLOTS + 8, 128), F32),
            jax.ShapeDtypeStruct((MODES, (LAST - FIRST) * TILE), BF16),
            jax.ShapeDtypeStruct((2 * BLOCKS, WIDE, 128), F32),
        ],
        in_specs=[pl.BlockSpec(memory_space=pltpu.HBM)] * 6,
        out_specs=[vmem, vmem, vmem],
        scratch_shapes=[
            pltpu.VMEM((SLOTS, MODES), BF16),
            pltpu.VMEM((1, SLOTS), BF16),
            pltpu.VMEM((1, SLOTS), jnp.int32),
            pltpu.VMEM((1, SLOTS), jnp.int32),
            pltpu.VMEM((1, SLOTS), jnp.int32),
            pltpu.VMEM((SLOTS + 8, 128), F32),
            pltpu.SemaphoreType.DMA,
            pltpu.SemaphoreType.DMA((5,)),
            pltpu.SemaphoreType.DMA((5,)),
            pltpu.SemaphoreType.DMA((5,)),
        ],
        compiler_params=pltpu.CompilerParams(
            collective_id=0, has_side_effects=True, vmem_limit_bytes=20 << 20
        ),
        name="gather_near",
    )(*(pltpu.with_memory_space_constraint(value, pltpu.HBM) for value in values))


def circle(phase):
    turns = phase * (0.5 / math.pi)
    part = turns - jnp.round(turns)
    square = part * part
    sine = SIN_TERMS[-1]
    for term in SIN_TERMS[-2::-1]:
        sine = sine * square + term
    sine = sine * part
    cosine = COS_TERMS[-1]
    for term in COS_TERMS[-2::-1]:
        cosine = cosine * square + term
    double = sine + sine
    return 1.0 - double * sine, double * cosine


TOGETHER = 56
STEPS_EACH = (LAST - FIRST) // 2 // TOGETHER
LISTED = NEAR // STEPS_EACH
TASKS = 8


def render_kernel(
    near, basis, clear, canvas, left, right, marks, slots, table, tasks, slots_sem, table_sem
):
    sector = lax.axis_index("sector")
    slab = lax.axis_index("slab")
    base_row = 2 * LINES * slab + LINES * sector
    slots_copy = pltpu.make_async_copy(near.at[:, :, pl.ds(SLOTS, 8)], slots, slots_sem)
    slots_copy.start()
    for hop in range(3):
        for side in range(2):
            tile_row, column, live = (
                near[hop, side, SLOTS + number : SLOTS + number + 1, :].astype(jnp.int32)
                for number in (1, 2, 3)
            )
            top = base_row - tile_row
            at = 2 * hop + side
            marks[at, 0:1, :] = top
            marks[at, 1:2, :] = column >> 7
            marks[at, 2:3, :] = column & 127
            for part in range(2):
                start = top + part * HALF
                reaches = (start >= 17 - (HALF - 1)) & (start <= 238) & (live > 0)
                marks[at, 3 + part : 4 + part, :] = reaches.astype(jnp.int32)
    table_copy = pltpu.make_async_copy(marks, table, table_sem)
    table_copy.start()
    coeff = [
        jnp.concatenate([near[hop, side, :SLOTS, :MODES] for side in range(2)], axis=0).astype(BF16)
        for hop in range(3)
    ]

    def form(part, step):
        mix = jnp.concatenate([coeff[2 * part], coeff[1]], axis=0)
        row = (part * STEPS_EACH + step) * TOGETHER
        columns = pl.ds(pl.multiple_of(row * TILE, TOGETHER * TILE), TOGETHER * TILE)
        phases = dot(mix, basis[:, columns])
        for extra in range(TOGETHER):
            place = pl.ds(pl.multiple_of((row + extra + FIRST + PAD) * WIDE, 8), 64)
            at = extra * TILE
            left[place, :] = phases[:, at : at + 128]
            right[place, :] = phases[:, at + 128 : at + 256]

    @pl.loop(0, STEPS_EACH)
    def _(step):
        form(0, step)

    table_copy.wait()
    slots_copy.wait()

    def form_and_list(step, count):
        form(1, step)
        for extra in range(LISTED):
            slot = step * LISTED + extra
            for part in range(2):
                tasks[count] = 2 * slot + part
                count = count + table[slot >> 4, 3 + part, slot & 15]
        return count

    count = lax.fori_loop(0, STEPS_EACH, form_and_list, 0)
    lane = lax.broadcasted_iota(jnp.int32, (1, 128), 1)
    down = lax.broadcasted_iota(jnp.int32, (HALF, 1), 0)
    reach = 7 * (TILE - 2)

    def tile_part(number):
        task = tasks[jnp.minimum(number, count - 1)]
        slot = task >> 1
        part = task & 1
        group = slot >> 4
        at = slot & 15
        weight = jnp.where(number < count, slots[slot >> 5, group & 1, 0, at], 0.0)
        top = table[group, 0, at] + part * HALF
        block = table[group, 1, at]
        shift = table[group, 2, at]
        start = (top + PAD) * WIDE + (slot & 63)
        vertical = jnp.abs(2 * (top + down) - (TILE - 1))
        vertical = jnp.where(8 * vertical <= reach, 4 * vertical, 4 * reach)
        vertical = jnp.broadcast_to(vertical, (HALF, 128))
        place = (lane - shift) & 127
        room_left = reach - 7 * ((TILE - 1) - 2 * place)
        room_right = reach - 7 * (2 * place + 1)
        both = []
        for ref, room in ((left, room_left), (right, room_right)):
            wave = pltpu.roll(ref[pl.ds(start, HALF, stride=WIDE), :], shift, 1)
            inside = vertical <= room
            amplitude = jnp.where(inside, weight, 0.0)
            cosine, sine = circle(jnp.where(inside, wave, 0.0))
            both.append((cosine * amplitude, sine * amplitude))
        rows = pl.ds(pl.multiple_of(part * HALF, HALF), HALF)
        return block, rows, jnp.broadcast_to(lane >= shift, (HALF, 128)), both

    def deposit(block, rows, kept, both):
        for comp in range(2):
            one, two = both[0][comp], both[1][comp]
            at = comp * BLOCKS + block
            past = jnp.minimum(at + 2, 2 * BLOCKS - 1)
            canvas[at, rows, :] += jnp.where(kept, one, 0.0)
            canvas[at + 1, rows, :] += jnp.where(kept, two, one)
            canvas[past, rows, :] += jnp.where(kept, 0.0, two)

    @pl.loop(0, (count + TASKS - 1) // TASKS)
    def _(step):
        before = None
        for extra in range(TASKS):
            piece = tile_part(TASKS * step + extra)
            if before is not None:
                deposit(*before)
            before = piece
        deposit(*before)


def render(near, basis, clear):
    vmem = pl.BlockSpec(memory_space=pltpu.VMEM)
    return pl.pallas_call(
        render_kernel,
        out_shape=jax.ShapeDtypeStruct((2 * BLOCKS, WIDE, 128), F32),
        in_specs=[vmem, vmem, vmem],
        out_specs=vmem,
        input_output_aliases={2: 0},
        scratch_shapes=[
            pltpu.VMEM(((TILE + 2 * PAD) * WIDE, 128), F32),
            pltpu.VMEM(((TILE + 2 * PAD) * WIDE, 128), F32),
            pltpu.VMEM((6, 8, 128), jnp.int32),
            pltpu.SMEM((3, 2, 8, 128), F32),
            pltpu.SMEM((6, 8, 128), jnp.int32),
            pltpu.SMEM((2 * NEAR + 8,), jnp.int32),
            pltpu.SemaphoreType.DMA,
            pltpu.SemaphoreType.DMA,
        ],
        compiler_params=pltpu.CompilerParams(vmem_limit_bytes=40 << 20),
        name="render_rows",
    )(near, basis, clear)


def encode(value):
    size = jnp.log(jnp.abs(value)) * (STEPS / math.log(2.0)) + (LOW * STEPS + 0.5)
    code = jnp.maximum(size, 0.0).astype(jnp.int32)
    return jnp.where(value < 0.0, -code, code)


def decode(code):
    size = jnp.abs(code).astype(F32) * (math.log(2.0) / STEPS) - LOW * math.log(2.0)
    value = jnp.exp(size)
    return jnp.where(code == 0, 0.0, jnp.where(code < 0, -value, value))


def exchange_kernel(
    field,
    turn,
    twist,
    long_turn,
    mid_ref,
    wide,
    box,
    handed,
    early,
    inbox,
    plain,
    send_sem,
    recv_sem,
    swap_send_sem,
    swap_recv_sem,
):
    sector = lax.axis_index("sector")
    slab = lax.axis_index("slab")
    other_sector = 1 - sector
    barrier = pltpu.get_barrier_semaphore()

    def greet(target):
        pl.semaphore_signal(barrier, inc=1, device_id=target, device_id_type=MESH)

    greet((other_sector, slab))

    @pl.loop(1, SLABS, unroll=21)
    def _(step):
        greet((sector, (slab + step) & (SLABS - 1)))

    def swap(chunk):
        return pltpu.make_async_remote_copy(
            src_ref=early.at[:, other_sector] if chunk == 0 else handed.at[chunk - 1],
            dst_ref=(inbox if chunk == 0 else box).at[chunk, :, sector],
            send_sem=swap_send_sem.at[chunk],
            recv_sem=swap_recv_sem.at[chunk],
            device_id=(other_sector, slab),
            device_id_type=MESH,
        )

    lines = field.reshape(2 * BLOCKS * WIDE, 128)
    codes = wide.reshape(DEVICES * SHORT, 128)
    values = plain.reshape(DEVICES * SHORT, 128)
    for chunk in range(CHUNKS):

        @pl.loop(0, CHUNK // 4)
        def _(step):
            parts = []
            for pair in range(2):
                line = chunk * CHUNK + 4 * step + 2 * pair
                both = [lines[pl.ds(line + e, 2 * BLOCKS, stride=WIDE), :] for e in range(2)]
                mid = dot_short(turn[...], jnp.concatenate(both, axis=1))
                for e in range(2):
                    real = mid[:64, 128 * e : 128 * e + 128]
                    imag = mid[64:, 128 * e : 128 * e + 128]
                    turned_real = real * twist[0] + imag * twist[1]
                    turned_imag = imag * twist[0] - real * twist[1]
                    parts.append(jnp.concatenate([turned_real, turned_imag], axis=1))
            done = encode(dot_long(jnp.concatenate(parts, axis=0), long_turn))
            for e in range(4):
                some = done[64 * e : 64 * e + 64]
                some = jnp.concatenate([some[:, :128], some[:, 128:]], axis=0).T
                codes[pl.ds(4 * step + e, DEVICES, stride=SHORT), :] = some

        @pl.loop(0, SLABS // 16)
        def _(step):
            some = pl.ds(step * 16, 16)
            for side, to in ((sector, sector), (other_sector, other_sector)):
                packed = wide[pl.ds(to * SLABS + step * 16, 16), :CHUNK].astype(jnp.int16)
                if chunk > 0 and side is other_sector:
                    handed[chunk - 1, some] = packed
                else:
                    box[chunk, some, side] = packed

        if chunk == 0:
            pl.semaphore_wait(barrier, SLABS)
        else:
            swap(chunk).start()
            swap(chunk).wait()
        land = early if chunk == 0 else inbox.at[chunk]

        @pl.loop(1, SLABS, unroll=3)
        def _(step):
            target = (slab + step) & (SLABS - 1)
            pltpu.make_async_remote_copy(
                src_ref=box.at[chunk, target],
                dst_ref=land.at[slab],
                send_sem=send_sem.at[chunk],
                recv_sem=recv_sem.at[chunk],
                device_id=(sector, target),
                device_id_type=MESH,
            ).start()

        land[slab] = box[chunk, slab]

    for chunk in range(CHUNKS):
        most = (early if chunk == 0 else inbox.at[chunk]).at[pl.ds(0, SLABS - 1)]
        pltpu.make_async_copy(most, most, recv_sem.at[chunk]).wait()
        if chunk == 0:
            swap(0).start()
            inbox[0, :, sector] = early[:, sector]
            swap(0).wait()

        @pl.loop(0, DEVICES // 16, unroll=4)
        def _(step):
            codes_in = inbox[chunk, pl.ds(step * 8, 8)].astype(jnp.int32)
            plain[pl.ds(step * 16, 16), :CHUNK] = decode(codes_in).reshape(16, CHUNK, 128)

        each = CHUNK if chunk == CHUNKS - 1 else 8

        @pl.loop(0, CHUNK // each)
        def _(step):
            parts = []
            for e in range(each):
                turned = values[pl.ds(each * step + e, DEVICES, stride=SHORT), :].T
                parts.append(jnp.concatenate([turned[:64], turned[64:]], axis=1))
            mid = dot_long(jnp.concatenate(parts, axis=0), long_turn)
            for e in range(each):
                line = chunk * CHUNK + each * step + e
                cos = twist[0, pl.ds(line, 1), :]
                sin = twist[1, pl.ds(line, 1), :]
                real = mid[64 * e : 64 * e + 64, :128]
                imag = mid[64 * e : 64 * e + 64, 128:]
                mid_ref[0, line, :LINES] = real * cos + imag * sin
                mid_ref[1, line, :LINES] = imag * cos - real * sin

    for chunk in range(CHUNKS):
        most = box.at[chunk, pl.ds(0, SLABS - 1)]
        pltpu.make_async_copy(most, most, send_sem.at[chunk]).wait()


def exchange(field, *consts):
    vmem = pl.BlockSpec(memory_space=pltpu.VMEM)
    return pl.pallas_call(
        exchange_kernel,
        out_shape=jax.ShapeDtypeStruct((2, LINES, WIDE, 128), F32),
        in_specs=[vmem] * 4,
        out_specs=vmem,
        scratch_shapes=[
            pltpu.VMEM((DEVICES, SHORT, 128), jnp.int32),
            pltpu.VMEM((CHUNKS, SLABS, 2, CHUNK, 128), jnp.int16),
            pltpu.VMEM((CHUNKS - 1, SLABS, CHUNK, 128), jnp.int16),
            pltpu.VMEM((SLABS, 2, CHUNK, 128), jnp.int16),
            pltpu.VMEM((CHUNKS, SLABS, 2, CHUNK, 128), jnp.int16),
            pltpu.VMEM((DEVICES, SHORT, 128), F32),
            pltpu.SemaphoreType.DMA((CHUNKS,)),
            pltpu.SemaphoreType.DMA((CHUNKS,)),
            pltpu.SemaphoreType.DMA((CHUNKS,)),
            pltpu.SemaphoreType.DMA((CHUNKS,)),
        ],
        compiler_params=pltpu.CompilerParams(
            collective_id=1, has_side_effects=True, vmem_limit_bytes=32 << 20
        ),
        name="exchange",
    )(field, *consts)


def finish_kernel(mid_ref, turn, out_hbm, turned, ready, out_sem):
    lines = mid_ref.reshape(2 * LINES * WIDE, 128)

    def leave(group):
        rows = pl.ds(group * 8, 8)
        return pltpu.make_async_copy(ready.at[:, rows], out_hbm.at[:, rows], out_sem.at[group])

    for group in range(LINES // 8):
        for pair in range(4):
            line = group * 8 + 2 * pair
            both = [lines[pl.ds(line + e, 2 * LINES, stride=WIDE), :] for e in range(2)]
            done = dot_short(turn[...], jnp.concatenate(both, axis=1))
            for e in range(2):
                turned[group % 2, pl.ds(2 * pair + e, 2 * LINES, stride=8), :] = done[
                    :, 128 * e : 128 * e + 128
                ]
        for comp in range(2):
            for block in range(LINES):
                at = (comp * LINES + block) * 8
                ready[comp, 8 * group : 8 * group + 8, 128 * block : 128 * block + 128] = turned[
                    group % 2, at : at + 8, :
                ]
        leave(group).start()
    for group in range(LINES // 8):
        leave(group).wait()


def finish(mid, turn):
    vmem = pl.BlockSpec(memory_space=pltpu.VMEM)
    return pl.pallas_call(
        finish_kernel,
        out_shape=jax.ShapeDtypeStruct((2, LINES, GRID), F32),
        in_specs=[vmem, vmem],
        out_specs=pl.BlockSpec(memory_space=pl.ANY),
        scratch_shapes=[
            pltpu.VMEM((2, 2 * LINES * 8, 128), F32),
            pltpu.VMEM((2, LINES, GRID), F32),
            pltpu.SemaphoreType.DMA((LINES // 8,)),
        ],
        compiler_params=pltpu.CompilerParams(vmem_limit_bytes=24 << 20),
        name="finish",
    )(mid, turn)


def body(mode_basis, mode_coeff, reflect, tile_row, tile_col, slot_live):
    turn, twist, long_turn, last_turn = (jnp.asarray(table) for table in tables())
    near, basis, clear = gather_near(
        mode_basis, mode_coeff, reflect, tile_row, tile_col, slot_live
    )
    field = render(near, basis, clear)
    mid = exchange(field, turn, twist, long_turn)
    return finish(mid, last_turn)


def solution(mesh):
    placed = (
        P(),
        P(("sector", "slab"), None),
        P(("sector", "slab")),
        P(("sector", "slab")),
        P(("sector", "slab")),
        P(("sector", "slab")),
    )
    return jax.shard_map(
        body,
        mesh=mesh,
        in_specs=placed,
        out_specs=P(None, ("sector", "slab"), None),
        check_vma=False,
    )
```

```python
import functools
import math

import jax
import jax.numpy as jnp
import ml_dtypes
import numpy as np
from jax import lax
from jax.experimental import pallas as pl
from jax.experimental.pallas import tpu as pltpu
from jax.sharding import PartitionSpec as P

GRID = 8192
TILE = 256
SLOTS = 16
MODES = 64
SLABS = 64
DEVICES = 128
LINES = GRID // DEVICES
BLOCKS = GRID // 128
NEAR = 6 * SLOTS
CHUNK = 16
CHUNKS = LINES // CHUNK
PAD = 16
HALF = 32
FIRST, LAST = 16, 240
WIDE = LINES + 8
SHORT = CHUNK + 8
MESH = pl.DeviceIdType.MESH
F32 = jnp.float32
BF16 = jnp.bfloat16

LOW = 12.0
STEPS = 32766.0 / (LOW + 15.25)


def polynomial(values, powers):
    spots = np.cos(np.pi * (np.arange(400) + 0.5) / 800) * 0.5
    table = np.stack([spots**power for power in powers], axis=1)
    return [float(c) for c in np.linalg.lstsq(table, values(np.pi * spots), rcond=None)[0]]


SIN_TERMS = polynomial(np.sin, (1, 3, 5, 7))
COS_TERMS = polynomial(np.cos, (0, 2, 4, 6))


def halves(table):
    high = table.astype(ml_dtypes.bfloat16)
    low = (table - high.astype(np.float64)).astype(ml_dtypes.bfloat16)
    return high, low


def angles(left, right, total):
    turns = np.outer(np.arange(left), np.arange(right)) % total
    return 2.0 * math.pi * turns / total


def stacked(table):
    high, low = halves(table)
    return np.block([[high, high], [low, np.zeros_like(low)]])


def tables():
    first = angles(64, 64, 64)
    turn = np.block([[np.cos(first), np.sin(first)], [-np.sin(first), np.cos(first)]])
    twist = angles(64, 128, GRID)
    second = angles(128, 128, 128)
    long_turn = np.block([[np.cos(second), -np.sin(second)], [np.sin(second), np.cos(second)]])
    return (
        stacked(turn),
        np.stack([np.cos(twist), np.sin(twist)]).astype(np.float32),
        np.stack(halves(long_turn)),
        stacked(turn / GRID),
    )


def split(value):
    high = value.astype(BF16)
    return high, (value - high.astype(F32)).astype(BF16)


def dot(left, right):
    return jnp.dot(left, right, preferred_element_type=F32)


def dot_short(table, value):
    high, low = split(value)
    both = dot(table, jnp.concatenate([high, low], axis=0))
    return both[:128] + both[128:]


def dot_long(value, tables):
    high, low = split(value)
    return dot(high, tables[0]) + dot(high, tables[1]) + dot(low, tables[0])


def gather_kernel(
    basis_hbm,
    coeff_hbm,
    reflect_hbm,
    row_hbm,
    column_hbm,
    live_hbm,
    near_ref,
    basis_ref,
    canvas_ref,
    coeff_ref,
    reflect_ref,
    row_ref,
    column_ref,
    live_ref,
    own,
    basis_sem,
    in_sem,
    send_sem,
    recv_sem,
):
    sector = lax.axis_index("sector")
    slab = lax.axis_index("slab")
    barrier = pltpu.get_barrier_semaphore()
    used = pl.ds(FIRST * TILE, (LAST - FIRST) * TILE)
    basis_copy = pltpu.make_async_copy(basis_hbm.at[:, used], basis_ref, basis_sem)
    sources = (coeff_hbm, reflect_hbm, row_hbm, column_hbm, live_hbm)
    held = (coeff_ref, reflect_ref, row_ref, column_ref, live_ref)
    loads = [
        pltpu.make_async_copy(one, two, in_sem.at[number])
        for number, (one, two) in enumerate(zip(sources, held))
    ]
    for load in loads:
        load.start()
    basis_copy.start()
    others = [(flip, hop) for hop in range(3) for flip in range(2)][1:]
    for flip, hop in others:
        for step in {hop, -hop}:
            pl.semaphore_signal(
                barrier,
                inc=1,
                device_id=(lax.rem(sector + flip, 2), lax.rem(slab + step + SLABS, SLABS)),
                device_id_type=MESH,
            )
    for load in loads:
        load.wait()
    own[:SLOTS, :MODES] = coeff_ref[...].astype(F32)
    for number, ref in enumerate((reflect_ref, row_ref, column_ref, live_ref)):
        own[SLOTS + number : SLOTS + number + 1, :SLOTS] = ref[...].astype(F32)
    near_ref[0, sector] = own[...]
    pl.semaphore_wait(barrier, 9)
    copies = []
    for number, (flip, hop) in enumerate(others):
        copy = pltpu.make_async_remote_copy(
            src_ref=own,
            dst_ref=near_ref.at[hop, sector],
            send_sem=send_sem.at[number],
            recv_sem=recv_sem.at[number],
            device_id=(lax.rem(sector + flip, 2), lax.rem(slab + hop, SLABS)),
            device_id_type=MESH,
        )
        copy.start()
        copies.append(copy)
    canvas_ref[...] = jnp.zeros_like(canvas_ref)
    for copy in copies:
        copy.wait()
    basis_copy.wait()


def gather_near(mode_basis, mode_coeff, *lists):
    vmem = pl.BlockSpec(memory_space=pltpu.VMEM)
    values = [mode_basis, mode_coeff] + [one.reshape(1, SLOTS) for one in lists]
    return pl.pallas_call(
        gather_kernel,
        out_shape=[
            jax.ShapeDtypeStruct((3, 2, SLOTS + 8, 128), F32),
            jax.ShapeDtypeStruct((MODES, (LAST - FIRST) * TILE), BF16),
            jax.ShapeDtypeStruct((2 * BLOCKS, WIDE, 128), F32),
        ],
        in_specs=[pl.BlockSpec(memory_space=pltpu.HBM)] * 6,
        out_specs=[vmem, vmem, vmem],
        scratch_shapes=[
            pltpu.VMEM((SLOTS, MODES), BF16),
            pltpu.VMEM((1, SLOTS), BF16),
            pltpu.VMEM((1, SLOTS), jnp.int32),
            pltpu.VMEM((1, SLOTS), jnp.int32),
            pltpu.VMEM((1, SLOTS), jnp.int32),
            pltpu.VMEM((SLOTS + 8, 128), F32),
            pltpu.SemaphoreType.DMA,
            pltpu.SemaphoreType.DMA((5,)),
            pltpu.SemaphoreType.DMA((5,)),
            pltpu.SemaphoreType.DMA((5,)),
        ],
        compiler_params=pltpu.CompilerParams(
            collective_id=0, has_side_effects=True, vmem_limit_bytes=20 << 20
        ),
        name="gather_near",
    )(*(pltpu.with_memory_space_constraint(value, pltpu.HBM) for value in values))


def circle(phase):
    turns = phase * (0.5 / math.pi)
    part = turns - jnp.round(turns)
    square = part * part
    sine = SIN_TERMS[-1]
    for term in SIN_TERMS[-2::-1]:
        sine = sine * square + term
    sine = sine * part
    cosine = COS_TERMS[-1]
    for term in COS_TERMS[-2::-1]:
        cosine = cosine * square + term
    double = sine + sine
    return 1.0 - double * sine, double * cosine


TOGETHER = 56
STEPS_EACH = (LAST - FIRST) // 2 // TOGETHER
LISTED = NEAR // STEPS_EACH
TASKS = 8


def render_kernel(
    near, basis, clear, canvas, left, right, marks, slots, table, tasks, slots_sem, table_sem
):
    sector = lax.axis_index("sector")
    slab = lax.axis_index("slab")
    base_row = 2 * LINES * slab + LINES * sector
    slots_copy = pltpu.make_async_copy(near.at[:, :, pl.ds(SLOTS, 8)], slots, slots_sem)
    slots_copy.start()
    for hop in range(3):
        for side in range(2):
            tile_row, column, live = (
                near[hop, side, SLOTS + number : SLOTS + number + 1, :].astype(jnp.int32)
                for number in (1, 2, 3)
            )
            top = base_row - tile_row
            at = 2 * hop + side
            marks[at, 0:1, :] = top
            marks[at, 1:2, :] = column >> 7
            marks[at, 2:3, :] = column & 127
            for part in range(2):
                start = top + part * HALF
                reaches = (start >= 17 - (HALF - 1)) & (start <= 238) & (live > 0)
                marks[at, 3 + part : 4 + part, :] = reaches.astype(jnp.int32)
    table_copy = pltpu.make_async_copy(marks, table, table_sem)
    table_copy.start()
    coeff = [
        jnp.concatenate([near[hop, side, :SLOTS, :MODES] for side in range(2)], axis=0).astype(BF16)
        for hop in range(3)
    ]

    def form(part, step):
        mix = jnp.concatenate([coeff[2 * part], coeff[1]], axis=0)
        row = (part * STEPS_EACH + step) * TOGETHER
        columns = pl.ds(pl.multiple_of(row * TILE, TOGETHER * TILE), TOGETHER * TILE)
        phases = dot(mix, basis[:, columns])
        for extra in range(TOGETHER):
            place = pl.ds(pl.multiple_of((row + extra + FIRST + PAD) * WIDE, 8), 64)
            at = extra * TILE
            left[place, :] = phases[:, at : at + 128]
            right[place, :] = phases[:, at + 128 : at + 256]

    @pl.loop(0, STEPS_EACH)
    def _(step):
        form(0, step)

    table_copy.wait()
    slots_copy.wait()

    def form_and_list(step, count):
        form(1, step)
        for extra in range(LISTED):
            slot = step * LISTED + extra
            for part in range(2):
                tasks[count] = 2 * slot + part
                count = count + table[slot >> 4, 3 + part, slot & 15]
        return count

    count = lax.fori_loop(0, STEPS_EACH, form_and_list, 0)
    lane = lax.broadcasted_iota(jnp.int32, (1, 128), 1)
    down = lax.broadcasted_iota(jnp.int32, (HALF, 1), 0)
    reach = 7 * (TILE - 2)

    def tile_part(number):
        task = tasks[jnp.minimum(number, count - 1)]
        slot = task >> 1
        part = task & 1
        group = slot >> 4
        at = slot & 15
        weight = jnp.where(number < count, slots[slot >> 5, group & 1, 0, at], 0.0)
        top = table[group, 0, at] + part * HALF
        block = table[group, 1, at]
        shift = table[group, 2, at]
        start = (top + PAD) * WIDE + (slot & 63)
        vertical = jnp.abs(2 * (top + down) - (TILE - 1))
        vertical = jnp.where(8 * vertical <= reach, 4 * vertical, 4 * reach)
        vertical = jnp.broadcast_to(vertical, (HALF, 128))
        place = (lane - shift) & 127
        room_left = reach - 7 * ((TILE - 1) - 2 * place)
        room_right = reach - 7 * (2 * place + 1)
        both = []
        for ref, room in ((left, room_left), (right, room_right)):
            wave = pltpu.roll(ref[pl.ds(start, HALF, stride=WIDE), :], shift, 1)
            inside = vertical <= room
            amplitude = jnp.where(inside, weight, 0.0)
            cosine, sine = circle(jnp.where(inside, wave, 0.0))
            both.append((cosine * amplitude, sine * amplitude))
        rows = pl.ds(pl.multiple_of(part * HALF, HALF), HALF)
        return block, rows, jnp.broadcast_to(lane >= shift, (HALF, 128)), both

    def deposit(block, rows, kept, both):
        for comp in range(2):
            one, two = both[0][comp], both[1][comp]
            at = comp * BLOCKS + block
            past = jnp.minimum(at + 2, 2 * BLOCKS - 1)
            canvas[at, rows, :] += jnp.where(kept, one, 0.0)
            canvas[at + 1, rows, :] += jnp.where(kept, two, one)
            canvas[past, rows, :] += jnp.where(kept, 0.0, two)

    @pl.loop(0, (count + TASKS - 1) // TASKS)
    def _(step):
        before = None
        for extra in range(TASKS):
            piece = tile_part(TASKS * step + extra)
            if before is not None:
                deposit(*before)
            before = piece
        deposit(*before)


def render(near, basis, clear):
    vmem = pl.BlockSpec(memory_space=pltpu.VMEM)
    return pl.pallas_call(
        render_kernel,
        out_shape=jax.ShapeDtypeStruct((2 * BLOCKS, WIDE, 128), F32),
        in_specs=[vmem, vmem, vmem],
        out_specs=vmem,
        input_output_aliases={2: 0},
        scratch_shapes=[
            pltpu.VMEM(((TILE + 2 * PAD) * WIDE, 128), F32),
            pltpu.VMEM(((TILE + 2 * PAD) * WIDE, 128), F32),
            pltpu.VMEM((6, 8, 128), jnp.int32),
            pltpu.SMEM((3, 2, 8, 128), F32),
            pltpu.SMEM((6, 8, 128), jnp.int32),
            pltpu.SMEM((2 * NEAR + 8,), jnp.int32),
            pltpu.SemaphoreType.DMA,
            pltpu.SemaphoreType.DMA,
        ],
        compiler_params=pltpu.CompilerParams(vmem_limit_bytes=40 << 20),
        name="render_rows",
    )(near, basis, clear)


def encode(value):
    size = jnp.log(jnp.abs(value)) * (STEPS / math.log(2.0)) + (LOW * STEPS + 0.5)
    code = jnp.maximum(size, 0.0).astype(jnp.int32)
    return jnp.where(value < 0.0, -code, code)


def decode(code):
    size = jnp.abs(code).astype(F32) * (math.log(2.0) / STEPS) - LOW * math.log(2.0)
    value = jnp.exp(size)
    return jnp.where(code == 0, 0.0, jnp.where(code < 0, -value, value))


def exchange_kernel(
    field,
    turn,
    twist,
    long_turn,
    mid_ref,
    wide,
    box,
    handed,
    early,
    inbox,
    plain,
    send_sem,
    recv_sem,
    swap_send_sem,
    swap_recv_sem,
):
    sector = lax.axis_index("sector")
    slab = lax.axis_index("slab")
    other_sector = 1 - sector
    barrier = pltpu.get_barrier_semaphore()

    def greet(target):
        pl.semaphore_signal(barrier, inc=1, device_id=target, device_id_type=MESH)

    greet((other_sector, slab))

    @pl.loop(1, SLABS, unroll=63)
    def _(step):
        greet((sector, (slab + step) & (SLABS - 1)))

    def swap(chunk):
        return pltpu.make_async_remote_copy(
            src_ref=early.at[:, other_sector] if chunk == 0 else handed.at[chunk - 1],
            dst_ref=(inbox if chunk == 0 else box).at[chunk, :, sector],
            send_sem=swap_send_sem.at[chunk],
            recv_sem=swap_recv_sem.at[chunk],
            device_id=(other_sector, slab),
            device_id_type=MESH,
        )

    lines = field.reshape(2 * BLOCKS * WIDE, 128)
    codes = wide.reshape(DEVICES * SHORT, 128)
    values = plain.reshape(DEVICES * SHORT, 128)
    for chunk in range(CHUNKS):

        @pl.loop(0, CHUNK // 4)
        def _(step):
            parts = []
            for pair in range(2):
                line = chunk * CHUNK + 4 * step + 2 * pair
                both = [lines[pl.ds(line + e, 2 * BLOCKS, stride=WIDE), :] for e in range(2)]
                mid = dot_short(turn[...], jnp.concatenate(both, axis=1))
                for e in range(2):
                    real = mid[:64, 128 * e : 128 * e + 128]
                    imag = mid[64:, 128 * e : 128 * e + 128]
                    turned_real = real * twist[0] + imag * twist[1]
                    turned_imag = imag * twist[0] - real * twist[1]
                    parts.append(jnp.concatenate([turned_real, turned_imag], axis=1))
            done = encode(dot_long(jnp.concatenate(parts, axis=0), long_turn))
            for e in range(4):
                some = done[64 * e : 64 * e + 64]
                some = jnp.concatenate([some[:, :128], some[:, 128:]], axis=0).T
                codes[pl.ds(4 * step + e, DEVICES, stride=SHORT), :] = some

        @pl.loop(0, SLABS // 16)
        def _(step):
            some = pl.ds(step * 16, 16)
            for side, to in ((sector, sector), (other_sector, other_sector)):
                packed = wide[pl.ds(to * SLABS + step * 16, 16), :CHUNK].astype(jnp.int16)
                if chunk > 0 and side is other_sector:
                    handed[chunk - 1, some] = packed
                else:
                    box[chunk, some, side] = packed

        if chunk == 0:
            pl.semaphore_wait(barrier, SLABS)
        else:
            swap(chunk).start()
            swap(chunk).wait()
        land = early if chunk == 0 else inbox.at[chunk]

        @pl.loop(1, SLABS, unroll=3)
        def _(step):
            target = (slab + step) & (SLABS - 1)
            pltpu.make_async_remote_copy(
                src_ref=box.at[chunk, target],
                dst_ref=land.at[slab],
                send_sem=send_sem.at[chunk],
                recv_sem=recv_sem.at[chunk],
                device_id=(sector, target),
                device_id_type=MESH,
            ).start()

        land[slab] = box[chunk, slab]

    for chunk in range(CHUNKS):
        most = (early if chunk == 0 else inbox.at[chunk]).at[pl.ds(0, SLABS - 1)]
        pltpu.make_async_copy(most, most, recv_sem.at[chunk]).wait()
        if chunk == 0:
            swap(0).start()
            inbox[0, :, sector] = early[:, sector]
            swap(0).wait()

        @pl.loop(0, DEVICES // 16, unroll=8 if chunk == CHUNKS - 1 else 4)
        def _(step):
            codes_in = inbox[chunk, pl.ds(step * 8, 8)].astype(jnp.int32)
            plain[pl.ds(step * 16, 16), :CHUNK] = decode(codes_in).reshape(16, CHUNK, 128)

        each = CHUNK if chunk == CHUNKS - 1 else 8

        @pl.loop(0, CHUNK // each)
        def _(step):
            parts = []
            for e in range(each):
                turned = values[pl.ds(each * step + e, DEVICES, stride=SHORT), :].T
                parts.append(jnp.concatenate([turned[:64], turned[64:]], axis=1))
            mid = dot_long(jnp.concatenate(parts, axis=0), long_turn)
            for e in range(each):
                line = chunk * CHUNK + each * step + e
                cos = twist[0, pl.ds(line, 1), :]
                sin = twist[1, pl.ds(line, 1), :]
                real = mid[64 * e : 64 * e + 64, :128]
                imag = mid[64 * e : 64 * e + 64, 128:]
                mid_ref[0, line, :LINES] = real * cos + imag * sin
                mid_ref[1, line, :LINES] = imag * cos - real * sin

    for chunk in range(CHUNKS):
        most = box.at[chunk, pl.ds(0, SLABS - 1)]
        pltpu.make_async_copy(most, most, send_sem.at[chunk]).wait()


def exchange(field, *consts):
    vmem = pl.BlockSpec(memory_space=pltpu.VMEM)
    return pl.pallas_call(
        exchange_kernel,
        out_shape=jax.ShapeDtypeStruct((2, LINES, WIDE, 128), F32),
        in_specs=[vmem] * 4,
        out_specs=vmem,
        scratch_shapes=[
            pltpu.VMEM((DEVICES, SHORT, 128), jnp.int32),
            pltpu.VMEM((CHUNKS, SLABS, 2, CHUNK, 128), jnp.int16),
            pltpu.VMEM((CHUNKS - 1, SLABS, CHUNK, 128), jnp.int16),
            pltpu.VMEM((SLABS, 2, CHUNK, 128), jnp.int16),
            pltpu.VMEM((CHUNKS, SLABS, 2, CHUNK, 128), jnp.int16),
            pltpu.VMEM((DEVICES, SHORT, 128), F32),
            pltpu.SemaphoreType.DMA((CHUNKS,)),
            pltpu.SemaphoreType.DMA((CHUNKS,)),
            pltpu.SemaphoreType.DMA((CHUNKS,)),
            pltpu.SemaphoreType.DMA((CHUNKS,)),
        ],
        compiler_params=pltpu.CompilerParams(
            collective_id=1, has_side_effects=True, vmem_limit_bytes=32 << 20
        ),
        name="exchange",
    )(field, *consts)


def finish_kernel(mid_ref, turn, out_hbm, turned, ready, out_sem):
    lines = mid_ref.reshape(2 * LINES * WIDE, 128)

    def leave(group):
        rows = pl.ds(group * 8, 8)
        return pltpu.make_async_copy(ready.at[:, rows], out_hbm.at[:, rows], out_sem.at[group])

    for group in range(LINES // 8):
        for pair in range(4):
            line = group * 8 + 2 * pair
            both = [lines[pl.ds(line + e, 2 * LINES, stride=WIDE), :] for e in range(2)]
            done = dot_short(turn[...], jnp.concatenate(both, axis=1))
            for e in range(2):
                turned[group % 2, pl.ds(2 * pair + e, 2 * LINES, stride=8), :] = done[
                    :, 128 * e : 128 * e + 128
                ]
        for comp in range(2):
            for block in range(LINES):
                at = (comp * LINES + block) * 8
                ready[comp, 8 * group : 8 * group + 8, 128 * block : 128 * block + 128] = turned[
                    group % 2, at : at + 8, :
                ]
        leave(group).start()
    for group in range(LINES // 8):
        leave(group).wait()


def finish(mid, turn):
    vmem = pl.BlockSpec(memory_space=pltpu.VMEM)
    return pl.pallas_call(
        finish_kernel,
        out_shape=jax.ShapeDtypeStruct((2, LINES, GRID), F32),
        in_specs=[vmem, vmem],
        out_specs=pl.BlockSpec(memory_space=pl.ANY),
        scratch_shapes=[
            pltpu.VMEM((2, 2 * LINES * 8, 128), F32),
            pltpu.VMEM((2, LINES, GRID), F32),
            pltpu.SemaphoreType.DMA((LINES // 8,)),
        ],
        compiler_params=pltpu.CompilerParams(vmem_limit_bytes=24 << 20),
        name="finish",
    )(mid, turn)


def body(mode_basis, mode_coeff, reflect, tile_row, tile_col, slot_live):
    turn, twist, long_turn, last_turn = (jnp.asarray(table) for table in tables())
    near, basis, clear = gather_near(
        mode_basis, mode_coeff, reflect, tile_row, tile_col, slot_live
    )
    field = render(near, basis, clear)
    mid = exchange(field, turn, twist, long_turn)
    return finish(mid, last_turn)


def solution(mesh):
    placed = (
        P(),
        P(("sector", "slab"), None),
        P(("sector", "slab")),
        P(("sector", "slab")),
        P(("sector", "slab")),
        P(("sector", "slab")),
    )
    return jax.shard_map(
        body,
        mesh=mesh,
        in_specs=placed,
        out_specs=P(None, ("sector", "slab"), None),
        check_vma=False,
    )
```
